256 devices in a mesh: rows: 256 (over y, x, z, core).
Axes of the slice: x: 4, y: 4, z: 8, core: 2. Of those that a mesh axis runs over, the one named last changes fastest.
Arguments:
- velocity: bfloat16 [131072, 8192], P('rows'), as said below
- basis_in: bfloat16 [131072, 256], P('rows'), may hold values from -0.015625 to 0.015625
Outputs:
- basis_out: float32 [131072, 256], P('rows')
- r_factor: float32 [256, 256], replicated
The draws below stay inside these ranges and needn't reach their ends.
Inputs may be any that keep to these rules, and one draw needn't show every extreme that they name: Entries of the velocity record lie within -15 and 15.
All inputs are finite; a program needn't handle non-finite values.
Results may differ from the reference program's by a relative error of at most 0.0029.
Values may be sent and summed in bfloat16 or wider, within the bound.
A program may use at most 128 MiB of HBM per device.

```python
import math
import jax
import jax.numpy as jnp
from jax import lax

SNAPS = 8192
RANK = 256
ROWS_DEV = 512
ROWS = 131072
N_ROWS = 256


def draw_velocity(key, part):
    key_base, key_rows, key_cols = jax.random.split(key, 3)
    base_values = jnp.clip(jax.random.normal(key_base, (ROWS, SNAPS), jnp.float32), -6.0, 6.0)
    row_scale = jnp.exp(jax.random.uniform(key_rows, (ROWS, 1), jnp.float32, 0.0, math.log(10.0)))
    position = jnp.arange(ROWS, dtype=jnp.float32)[:, None] / ROWS
    rising = jnp.exp(math.log(3.0) * position)
    col_scale = jnp.exp(jax.random.uniform(key_cols, (1, SNAPS), jnp.float32, 0.0, math.log(4.0)))
    return (0.02 * base_values * row_scale * rising * col_scale).astype(jnp.bfloat16)


def levels(stream_key, extent, cuts, smallest, high):
    loudness = 1.0
    for dim, shards_of in cuts:
        draws = jax.random.uniform(jax.random.fold_in(jax.random.fold_in(stream_key, 6), dim), (shards_of,), jnp.float32, smallest / len(cuts), high / len(cuts))
        loudness = loudness * jnp.repeat(jnp.exp(draws), extent[dim] // shards_of).reshape((-1,) + (1,) * (len(extent) - 1 - dim))
    return loudness


def centred(rng, shape, spread, bound, pieces=(), kind=jnp.bfloat16):
    factor_of = levels(rng, shape, pieces, -0.22, 0.18) if pieces else 1.0
    entries = jax.random.normal(rng, shape, jnp.float32) * spread * factor_of
    return jnp.minimum(jnp.maximum(entries, -bound), bound).astype(kind)


def setup_inputs(seed: int = 0) -> dict:
    splits = jax.random.split(jax.random.key(seed), 3)
    return {
        "velocity": draw_velocity(jax.random.fold_in(splits[2], 71), 0),
        "basis_in": centred(splits[1], (ROWS, RANK), ROWS ** -0.5, 0.015625, ((0, 256),)),
    }


def reference(velocity, basis_in):
    blocks = velocity.reshape(N_ROWS, ROWS_DEV, SNAPS)
    basis_blocks = basis_in.reshape(N_ROWS, ROWS_DEV, RANK)

    def add_block(running, pair):
        columns, basis_rows = pair
        term = lax.dot_general(columns.astype(jnp.float32), basis_rows.astype(jnp.float32), (((0,), (0,)), ((), ())), preferred_element_type=jnp.float32)
        return (running + term, None)
    start_sum = jnp.zeros((SNAPS, RANK), jnp.float32)
    coefficients, _unused = lax.scan(add_block, start_sum, (blocks, basis_blocks))
    coefficients_bf = coefficients.astype(jnp.bfloat16)

    def project(columns):
        return jnp.dot(columns.astype(jnp.float32), coefficients_bf.astype(jnp.float32), preferred_element_type=jnp.float32)
    projected = lax.map(project, blocks).reshape(ROWS, RANK)
    q_part, r_part = jnp.linalg.qr(projected)
    signs = jnp.sign(jnp.diagonal(r_part))
    upper = r_part * signs[:, None]
    ortho = q_part * signs[None, :]
    norm_scale = jnp.sqrt(jnp.float32(ROWS))
    return (ortho * norm_scale, upper / norm_scale)
```

```python
import functools

import jax
import jax.numpy as jnp
from jax import lax
from jax.experimental import pallas as pl
from jax.experimental.pallas import tpu as pltpu
from jax.sharding import PartitionSpec as P

NY, NX, NZ = 4, 4, 8
SIZE = {"x": NX, "z": NZ, "y": NY}
PLACE = {"x": 0, "z": 1, "y": 2}
MESH = pl.DeviceIdType.MESH
HIGHEST = lax.Precision.HIGHEST

RS_PARTS = ((0, 24, "xyz"), (24, 24, "yzx"), (48, 16, "zxy"))
AG_PARTS = ((0, 32, "zyx"), (32, 16, "xzy"), (48, 16, "yxz"))


def dot(a, b, contract, precision=None):
    return lax.dot_general(
        a, b, ((contract[:1], contract[1:]), ((), ())),
        precision=precision, preferred_element_type=jnp.float32,
    )


def block_of(at, first, rows, full, fixed, split=None):
    index = [None, None, None]
    for axis in "xzy":
        place = PLACE[axis]
        if axis in fixed:
            index[place] = pl.ds(fixed[axis], 1)
        else:
            index[place] = pl.ds(0, SIZE[axis])
    if split is not None and split[0] == "row":
        first, rows = first + split[1], split[2]
    elif split is not None:
        index[PLACE[split[0]]] = pl.ds(split[1], split[2])
    return at[tuple(index) + (pl.ds(first, rows), slice(None))]


def halves_of(rows, whole_axes, granule):
    if whole_axes:
        axis = whole_axes[0]
        half = SIZE[axis] // 2
        return ((axis, 0, half), (axis, half, half))
    if rows >= 2 * granule:
        upper = rows // 2 // granule * granule
        return (("row", 0, upper), ("row", upper, rows - upper))
    return (("row", 0, rows), None)


def block_shape(rows, whole_axes, split):
    shape = [1, 1, 1]
    for axis in whole_axes:
        shape[PLACE[axis]] = SIZE[axis]
    if split is not None and split[0] == "row":
        rows = split[2]
    elif split is not None:
        shape[PLACE[split[0]]] = split[2]
    return tuple(shape) + (rows, 128)


def rs_messages():
    messages = []
    for part, (first, rows, order) in enumerate(RS_PARTS):
        for stage, axis in enumerate(order):
            rest = order[stage + 1:]
            halves = halves_of(rows, rest, 8)
            for step in range(1, SIZE[axis] // 2 + 1):
                for way in (0, 1):
                    split = halves[way] if step == 1 else None
                    messages.append(((part, stage, step, way), block_shape(rows, rest, split)))
    return messages


RS_MESSAGES = rs_messages()
RS_SLOT = {key: slot for slot, (key, _) in enumerate(RS_MESSAGES)}
N_RS = len(RS_MESSAGES)
N_AG = 64
N_SIB = 64


def exchange_kernel(*refs):
    v_hbm, b_hbm, p_ref, g_ref = refs[:4]
    (v, v_sib, b, b_sib, total, gathered, gram_in, gram_chip, gram_parts, gram_z, gram_row) = refs[4:15]
    received = refs[15:15 + N_RS]
    (load_sem, sib_send, sib_recv, rs_send, rs_recv, ag_send, ag_recv,
     fwd_send, fwd_recv, gx_send, gx_recv) = refs[15 + N_RS:]

    me = lax.axis_index("rows")
    core = me % 2
    mine = {"z": me // 2 % NZ, "x": me // (2 * NZ) % NX, "y": me // (2 * NZ * NX)}

    def device(**moved):
        at = {**mine, "core": core, **moved}
        return (((at["y"] * NX + at["x"]) * NZ + at["z"]) * 2 + at["core"],)

    def along(axis, offset):
        return (mine[axis] + offset + SIZE[axis]) % SIZE[axis]

    sibling = device(core=1 - core)

    def remote(source, target, send, recv, to):
        return pltpu.make_async_remote_copy(
            src_ref=source, dst_ref=target, send_sem=send, recv_sem=recv,
            device_id=to, device_id_type=MESH,
        )

    half = v_sib.shape[1]
    wide = half // NX

    def columns(which_core, k):
        return pl.ds(pl.multiple_of(which_core * half + k * wide, 128), wide)

    loads = []
    for n, (which, k) in enumerate([(core, k) for k in range(NX)] + [(1 - core, k) for k in range(NX)]):
        loads.append(pltpu.make_async_copy(
            v_hbm.at[:, columns(which, k)], v.at[:, columns(which, k)], load_sem.at[n]))
    load_b = pltpu.make_async_copy(b_hbm, b, load_sem.at[2 * NX])
    load_b.start()
    for load in loads:
        load.start()

    partners = [sibling]
    for dy in range(NY):
        for dx in range(NX):
            if dy or dx:
                partners.append(device(y=along("y", dy), x=along("x", dx)))
    for dz in range(1, NZ):
        partners.append(device(z=along("z", dz)))
    barrier = pltpu.get_barrier_semaphore()
    for partner in partners:
        pl.semaphore_signal(barrier, inc=1, device_id=partner, device_id_type=MESH)
    pl.semaphore_wait(barrier, len(partners))

    sends = []

    copy_b = remote(b_hbm, b_sib, sib_send.at[NX], sib_recv.at[NX], sibling)
    copy_b.start()
    copies_v = []
    for k in range(NX):
        copy = remote(
            v_hbm.at[:, columns(1 - core, k)], v_sib.at[:, pl.ds(k * wide, wide)],
            sib_send.at[k], sib_recv.at[k], sibling)
        copy.start()
        copies_v.append(copy)
    sends += copies_v + [copy_b]

    load_b.wait()
    copy_b.wait_recv()
    b_t = b[...].T
    b_sib_t = b_sib[...].T
    for k in range(NX):
        loads[k].wait()
        copies_v[k].wait_recv()
        product = dot(b_t, v[:, columns(core, k)], (1, 0))
        product += dot(b_sib_t, v_sib[:, k * wide:(k + 1) * wide], (1, 0))
        for n in range(NZ):
            total[k, n] = product[:, n * 128:(n + 1) * 128].reshape(NY, 64, 128)

    def rs_block(part, stage, target, split=None):
        first, rows, order = RS_PARTS[part]
        axis = order[stage]
        fixed = {done: mine[done] for done in order[:stage]}
        fixed[axis] = target
        return block_of(total.at, first, rows, order[stage + 1:], fixed, split)

    def rs_copy(part, stage, step, way):
        first, rows, order = RS_PARTS[part]
        axis = order[stage]
        sign = 1 - 2 * way
        target = along(axis, sign * (SIZE[axis] // 2 - step + 1))
        split = halves_of(rows, order[stage + 1:], 8)[way] if step == 1 else None
        slot = RS_SLOT[part, stage, step, way]
        return remote(
            rs_block(part, stage, target, split), received[slot], rs_send.at[slot], rs_recv.at[slot],
            device(**{axis: along(axis, sign)}))

    def rs_start(part, stage, step):
        for way in (0, 1):
            copy = rs_copy(part, stage, step, way)
            copy.start()
            sends.append(copy)

    def rs_finish(part, stage, step):
        first, rows, order = RS_PARTS[part]
        axis = order[stage]
        for way in (0, 1):
            sign = 1 - 2 * way
            slot = RS_SLOT[part, stage, step, way]
            rs_copy(part, stage, step, way).wait_recv()
            target = along(axis, sign * (SIZE[axis] // 2 - step))
            split = halves_of(rows, order[stage + 1:], 8)[way] if step == 1 else None
            block = rs_block(part, stage, target, split)
            block[...] = block[...] + received[slot][...]

    steps = []
    for first, rows, order in RS_PARTS:
        steps.append([(stage, step) for stage, axis in enumerate(order) for step in range(1, SIZE[axis] // 2 + 1)])
    for part in (0, 1, 2):
        rs_start(part, *steps[part][0])
    for turn in range(len(steps[0])):
        for part in (2, 0, 1):
            rs_finish(part, *steps[part][turn])
            if turn + 1 < len(steps[part]):
                rs_start(part, *steps[part][turn + 1])

    own = total[pl.ds(mine["x"], 1), pl.ds(mine["z"], 1), pl.ds(mine["y"], 1)]
    gathered[pl.ds(core, 1), pl.ds(mine["x"], 1), pl.ds(mine["z"], 1), pl.ds(mine["y"], 1)] = (
        own.astype(jnp.bfloat16)[None])

    def ag_block(part, stage, origin, split=None, whole_stage=False):
        first, rows, order = AG_PARTS[part]
        axis = order[stage]
        fixed = {later: mine[later] for later in order[stage + 1:]}
        if not whole_stage:
            fixed[axis] = origin
        return block_of(gathered.at[core].at, first, rows, order[:stage], fixed, split)

    counters = {"ag": 0, "fwd": 0}

    def forward(ref):
        slot = counters["fwd"]
        counters["fwd"] += 1
        copy = remote(ref, ref, fwd_send.at[slot], fwd_recv.at[slot], sibling)
        copy.start()
        sends.append(copy)
        return slot

    def sibling_block(part, stage, origin, split):
        first, rows, order = AG_PARTS[part]
        axis = order[stage]
        fixed = {axis: origin}
        return block_of(gathered.at[1 - core].at, first, rows, order[:stage], fixed, split)

    forwarded = []
    pending = {}

    def ag_start(part, stage, step):
        first, rows, order = AG_PARTS[part]
        axis = order[stage]
        last = step == SIZE[axis] // 2
        halves = halves_of(rows, order[:stage], 16)
        if stage == 2 and step == 1:
            slot = forward(ag_block(part, stage, mine[axis]))
            forwarded.append((slot, part, stage, mine[axis], None))
        for way in (0, 1):
            sign = 1 - 2 * way
            split = halves[way] if last else None
            if last and split is None:
                continue
            block = ag_block(part, stage, along(axis, -sign * (step - 1)), split)
            slot = counters["ag"]
            counters["ag"] += 1
            copy = remote(block, block, ag_send.at[slot], ag_recv.at[slot], device(**{axis: along(axis, sign)}))
            copy.start()
            sends.append(copy)
            arriving = ag_block(part, stage, along(axis, -sign * step), split)
            pending[part, stage, step, way] = (slot, arriving, along(axis, -sign * step), split)

    def ag_finish(part, stage, step):
        first, rows, order = AG_PARTS[part]
        axis = order[stage]
        for way in (0, 1):
            if (part, stage, step, way) not in pending:
                continue
            slot, arriving, origin, split = pending[part, stage, step, way]
            remote(arriving, arriving, ag_send.at[slot], ag_recv.at[slot], sibling).wait_recv()
            if stage == 2:
                slot = forward(arriving)
                forwarded.append((slot, part, stage, origin, split))

    steps = []
    for first, rows, order in AG_PARTS:
        steps.append([(stage, step) for stage, axis in enumerate(order) for step in range(1, SIZE[axis] // 2 + 1)])
    for part in (0, 1, 2):
        ag_start(part, *steps[part][0])
    for turn in range(len(steps[0])):
        for part in (0, 1, 2):
            ag_finish(part, *steps[part][turn])
            if turn + 1 < len(steps[part]):
                ag_start(part, *steps[part][turn + 1])
    for slot, part, stage, origin, split in forwarded:
        block = sibling_block(part, stage, origin, split)
        remote(block, block, fwd_send.at[slot], fwd_recv.at[slot], sibling).wait_recv()

    for load in loads[NX:]:
        load.wait()
    projected = None
    for which in range(2):
        for k in range(NX):
            block = jnp.concatenate([gathered[which, k, n].reshape(256, 128) for n in range(NZ)], axis=1)
            term = dot(v[:, which * half + k * wide:which * half + (k + 1) * wide], block, (1, 1))
            projected = term if projected is None else projected + term
    p_ref[...] = projected
    gram_in[0] = dot(projected, projected, (0, 0), HIGHEST)

    copy = remote(gram_in.at[0], gram_in.at[1], gx_send.at[0], gx_recv.at[0], sibling)
    copy.start()
    sends.append(copy)
    copy.wait_recv()
    gram_chip[...] = (gram_in[0] + gram_in[1]).reshape(2, NY, NX, 8, 256)

    plane = [(dy, dx) for dy in range(NY) for dx in range(NX) if dy or dx]
    scatter = []
    for n, (dy, dx) in enumerate(plane):
        y, x = along("y", dy), along("x", dx)
        copy = remote(
            gram_chip.at[core, y, x], gram_parts.at[n], gx_send.at[1 + n], gx_recv.at[1 + n], device(y=y, x=x))
        copy.start()
        scatter.append(copy)
    sends += scatter
    row = gram_chip[core, mine["y"], mine["x"]]
    for n, copy in enumerate(scatter):
        copy.wait_recv()
        row += gram_parts[n]
    gram_z[mine["z"]] = row
    spread = []
    for dz in range(1, NZ):
        slot = 16 + dz
        z = along("z", dz)
        copy = remote(
            gram_z.at[mine["z"]], gram_z.at[mine["z"]], gx_send.at[slot], gx_recv.at[slot], device(z=z))
        copy.start()
        sends.append(copy)
    for dz in range(1, NZ):
        slot = 16 + dz
        z = along("z", -dz)
        remote(gram_z.at[z], gram_z.at[z], gx_send.at[slot], gx_recv.at[slot], sibling).wait_recv()
    row = gram_z[0]
    for n in range(1, NZ):
        row += gram_z[n]
    gram_row[core, mine["y"], mine["x"]] = row
    for n, (dy, dx) in enumerate(plane):
        slot = 24 + n
        here = gram_row.at[core, mine["y"], mine["x"]]
        copy = remote(
            here, here, gx_send.at[slot], gx_recv.at[slot], device(y=along("y", dy), x=along("x", dx)))
        copy.start()
        sends.append(copy)
    for n, (dy, dx) in enumerate(plane):
        slot = 24 + n
        there = gram_row.at[core, along("y", -dy), along("x", -dx)]
        remote(there, there, gx_send.at[slot], gx_recv.at[slot], sibling).wait_recv()
    copy = remote(gram_row.at[core], gram_row.at[core], gx_send.at[40], gx_recv.at[40], sibling)
    copy.start()
    sends.append(copy)
    arriving = gram_row.at[1 - core]
    remote(arriving, arriving, gx_send.at[40], gx_recv.at[40], sibling).wait_recv()
    g_ref[...] = gram_row[...].reshape(256, 256)
    for copy in sends:
        copy.wait_send()


def exchange(velocity, basis_in):
    rows, snaps = velocity.shape
    rank = basis_in.shape[1]
    f32, bf16 = jnp.float32, jnp.bfloat16
    dma = pltpu.SemaphoreType.DMA
    return pl.pallas_call(
        exchange_kernel,
        out_shape=(
            jax.ShapeDtypeStruct((rows, rank), f32),
            jax.ShapeDtypeStruct((rank, rank), f32),
        ),
        in_specs=[pl.BlockSpec(memory_space=pl.ANY)] * 2,
        out_specs=[pl.BlockSpec(memory_space=pltpu.VMEM)] * 2,
        scratch_shapes=[
            pltpu.VMEM((rows, snaps), bf16),
            pltpu.VMEM((rows, snaps // 2), bf16),
            pltpu.VMEM((rows, rank), bf16),
            pltpu.VMEM((rows, rank), bf16),
            pltpu.VMEM((NX, NZ, NY, 64, 128), f32),
            pltpu.VMEM((2, NX, NZ, NY, 64, 128), bf16),
            pltpu.VMEM((2, rank, rank), f32),
            pltpu.VMEM((2, NY, NX, 8, rank), f32),
            pltpu.VMEM((NY * NX - 1, 8, rank), f32),
            pltpu.VMEM((NZ, 8, rank), f32),
            pltpu.VMEM((2, NY, NX, 8, rank), f32),
            *[pltpu.VMEM(shape, f32) for _, shape in RS_MESSAGES],
            dma((2 * NX + 1,)),
            dma((NX + 1,)),
            dma((NX + 1,)),
            dma((N_RS,)),
            dma((N_RS,)),
            dma((N_AG,)),
            dma((N_AG,)),
            dma((N_SIB,)),
            dma((N_SIB,)),
            dma((41,)),
            dma((41,)),
        ],
        compiler_params=pltpu.CompilerParams(
            collective_id=0, has_side_effects=True, vmem_limit_bytes=56 * 2**20
        ),
        cost_estimate=pl.CostEstimate(
            flops=4 * rows * snaps * rank, bytes_accessed=2 * rows * snaps, transcendentals=0
        ),
    )(velocity, basis_in)


def factor_kernel(scale, p_ref, g_ref, out_ref, r_ref, w, state):
    size = g_ref.shape[0]
    row = lax.broadcasted_iota(jnp.int32, (size, size), 0)
    col = lax.broadcasted_iota(jnp.int32, (size, size), 1)
    eye = (row == col).astype(jnp.float32)
    weight = jnp.where(row < col, 1.0, 0.5 * eye)
    gram = g_ref[...]
    diagonal = gram * eye
    unit_row = lax.rsqrt(jnp.sum(diagonal, axis=0, keepdims=True))
    unit_col = lax.rsqrt(jnp.sum(diagonal, axis=1, keepdims=True))
    scaled = gram * unit_row * unit_col

    w[...] = eye
    state[...] = scaled - eye

    def go_on(carry):
        count, norm = carry
        return (norm > 1e-6) & (norm < 1e4) & (count < 12)

    def improve():
        upper = state[...] * weight
        once = dot(w[...], upper, (1, 0), HIGHEST)
        w[...] = w[...] - once + dot(once, upper, (1, 0), HIGHEST)

    def step(carry):
        count, _ = carry
        improve()
        excess = dot(w[...], dot(scaled, w[...], (1, 0), HIGHEST), (0, 0), HIGHEST) - eye
        state[...] = excess
        return count + 1, jnp.sum(excess * excess)

    start = state[...]
    _, norm = lax.while_loop(go_on, step, (0, jnp.sum(start * start)))
    converged = norm <= 1e-6

    @pl.when(converged)
    def _():
        improve()

    @pl.when(jnp.logical_not(converged))
    def _():
        state[...] = scaled
        r_ref[...] = jnp.zeros_like(r_ref)
        lane = lax.broadcasted_iota(jnp.int32, (1, size), 1)

        def eliminate(j, _):
            pivot_row = jnp.where(lane >= j, state[pl.ds(j, 1), :], 0.0)
            pivot = jnp.sum(jnp.where(lane == j, pivot_row, 0.0), axis=1, keepdims=True)
            pivot_row = pivot_row / jnp.sqrt(pivot)
            r_ref[pl.ds(j, 1), :] = pivot_row
            pivot_col = jnp.sum(jnp.broadcast_to(pivot_row, (size, size)) * eye, axis=1, keepdims=True)
            state[...] = state[...] - pivot_col * pivot_row
            return 0

        lax.fori_loop(0, size, eliminate, 0)
        w[...] = jnp.zeros_like(w)

        def substitute(n, _):
            j = size - 1 - n
            line = r_ref[pl.ds(j, 1), :]
            pivot = jnp.sum(jnp.where(lane == j, line, 0.0), axis=1, keepdims=True)
            beyond = jnp.where(lane > j, line, 0.0)
            unit = jnp.where(lane == j, 1.0, 0.0)
            w[pl.ds(j, 1), :] = (unit - dot(beyond, w[...], (1, 0), HIGHEST)) / pivot
            return 0

        lax.fori_loop(0, size, substitute, 0)

    triangle = jnp.where(row <= col, dot(w[...], scaled, (0, 0), HIGHEST), 0.0)
    r_ref[...] = triangle / unit_row / scale
    out_ref[...] = dot(p_ref[...], w[...] * unit_col * scale, (1, 0), HIGHEST)


def factor(projected, gram, scale):
    rank = gram.shape[0]
    return pl.pallas_call(
        functools.partial(factor_kernel, scale),
        out_shape=(
            jax.ShapeDtypeStruct(projected.shape, jnp.float32),
            jax.ShapeDtypeStruct((rank, rank), jnp.float32),
        ),
        scratch_shapes=[pltpu.VMEM((rank, rank), jnp.float32)] * 2,
        compiler_params=pltpu.CompilerParams(vmem_limit_bytes=32 * 2**20),
    )(projected, gram)


def local(velocity, basis_in):
    projected, gram = exchange(velocity, basis_in)
    scale = float(lax.axis_size("rows") * velocity.shape[0]) ** 0.5
    return factor(projected, gram, scale)


def solution(mesh):
    in_specs = (P("rows", None), P("rows", None))
    out_specs = (P("rows", None), P())
    return jax.shard_map(local, mesh=mesh, in_specs=in_specs, out_specs=out_specs, check_vma=False)
```

```python
import functools

import jax
import jax.numpy as jnp
from jax import lax
from jax.experimental import pallas as pl
from jax.experimental.pallas import tpu as pltpu
from jax.sharding import PartitionSpec as P

NY, NX, NZ = 4, 4, 8
SIZE = {"x": NX, "z": NZ, "y": NY}
MESH = pl.DeviceIdType.MESH
HIGHEST = lax.Precision.HIGHEST


PARTS = (("x", "y"), ("y", "x"))
PIECE = 32
FAR_FIRST = (2, 1, 3)
SCALE = 2.0**17


def dot(a, b, contract, precision=None):
    return lax.dot_general(
        a, b, ((contract[:1], contract[1:]), ((), ())),
        precision=precision, preferred_element_type=jnp.float32,
    )


def encode(value):
    scaled = value * SCALE
    return (scaled * scaled * (scaled * jnp.abs(scaled))).astype(jnp.bfloat16)


def decode(code):
    wide = code.astype(jnp.float32)
    power = jnp.maximum(jnp.abs(wide), 1e-37)
    root = lax.rsqrt(power)
    return wide * root * (lax.rsqrt(power * root) * (1.0 / SCALE))


def exchange_kernel(
    v_hbm, b_hbm, p_ref, g_ref,
    v, v_sib, b, b_sib, total, coded, in_first, in_second, in_z, gathered,
    gram_in, gram_chip, gram_parts, gram_z, gram_row,
    load_sem, sib_send, sib_recv, first_send, first_recv, second_send, second_recv,
    z_send, z_recv, out_z_send, out_z_recv, out_second_send, out_second_recv,
    out_first_send, out_first_recv, fwd_send, fwd_recv, gx_send, gx_recv,
):
    me = lax.axis_index("rows")
    core = me % 2
    mine = {"z": me // 2 % NZ, "x": me // (2 * NZ) % NX, "y": me // (2 * NZ * NX)}

    def device(**moved):
        at = {**mine, "core": core, **moved}
        return (((at["y"] * NX + at["x"]) * NZ + at["z"]) * 2 + at["core"],)

    def along(axis, offset):
        return (mine[axis] + offset + SIZE[axis]) % SIZE[axis]

    sibling = device(core=1 - core)

    def remote(source, target, send, recv, to):
        return pltpu.make_async_remote_copy(
            src_ref=source, dst_ref=target, send_sem=send, recv_sem=recv,
            device_id=to, device_id_type=MESH,
        )

    sends = []

    def start(copy):
        copy.start()
        sends.append(copy)

    half = v_sib.shape[1]
    wide = half // NX

    def columns(which_core, k):
        return pl.ds(pl.multiple_of(which_core * half + k * wide, 128), wide)

    order = [along("x", offset) for offset in FAR_FIRST + (0,)]
    loads = []
    for n, (which, k) in enumerate([(core, k) for k in order] + [(1 - core, k) for k in range(NX)]):
        loads.append(pltpu.make_async_copy(
            v_hbm.at[:, columns(which, k)], v.at[:, columns(which, k)], load_sem.at[n]))
    load_b = pltpu.make_async_copy(b_hbm, b, load_sem.at[2 * NX])
    load_b.start()
    for load in loads:
        load.start()

    partners = [sibling]
    for dy in range(NY):
        for dx in range(NX):
            if dy or dx:
                partners.append(device(y=along("y", dy), x=along("x", dx)))
    for dz in range(1, NZ):
        partners.append(device(z=along("z", dz)))
    barrier = pltpu.get_barrier_semaphore()
    for partner in partners:
        pl.semaphore_signal(barrier, inc=1, device_id=partner, device_id_type=MESH)
    pl.semaphore_wait(barrier, len(partners))

    copy_b = remote(b_hbm, b_sib, sib_send.at[NX], sib_recv.at[NX], sibling)
    start(copy_b)
    copies_v = []
    for n, k in enumerate(order):
        copy = remote(
            v_hbm.at[:, columns(1 - core, k)], v_sib.at[:, pl.ds(n * wide, wide)],
            sib_send.at[n], sib_recv.at[n], sibling)
        start(copy)
        copies_v.append(copy)

    load_b.wait()
    b_t = b[...].T
    copy_b.wait_recv()
    b_sib_t = b_sib[...].T

    def first_copy(part, away, o2):
        first, _ = PARTS[part]
        k = along(first, away)
        slot = (away - 1) * 4 + o2
        return remote(
            coded.at[part, k, o2], in_first.at[part, away - 1, o2],
            first_send.at[part, slot], first_recv.at[part, slot], device(**{first: k}))

    for n, k in enumerate(order):
        loads[n].wait()
        copies_v[n].wait_recv()
        product = dot(b_t, v[:, columns(core, k)], (1, 0))
        product += dot(b_sib_t, v_sib[:, n * wide:(n + 1) * wide], (1, 0))
        for part in range(2):
            for o2 in range(4):
                ranks = slice(part * 128 + o2 * PIECE, part * 128 + (o2 + 1) * PIECE)
                for z in range(NZ):
                    tile = product[ranks, z * 128:(z + 1) * 128]
                    total[part, k, o2, z] = tile
                    coded[part, k, o2, z] = encode(tile)
        for j2 in FAR_FIRST + (0,):
            if n < 3:
                first_copy(0, FAR_FIRST[n], along("y", j2)).start()
        away = (k - mine["y"] + NY) % NY

        @pl.when(away != 0)
        def _():
            for j2 in FAR_FIRST + (0,):
                first_copy(1, away, along("x", j2)).start()

    sums = [None, None]
    for j2 in FAR_FIRST + (0,):
        for part, (first, second) in enumerate(PARTS):
            o2 = along(second, j2)
            block = total[part, mine[first], o2]
            for away in (2, 1, 3):
                first_copy(part, away, o2).wait_recv()
                block += decode(in_first[part, away - 1, o2])
            if j2:
                coded[part, mine[first], o2] = encode(block)
                start(remote(
                    coded.at[part, mine[first], o2], in_second.at[part, j2 - 1],
                    second_send.at[part, j2 - 1], second_recv.at[part, j2 - 1], device(**{second: o2})))
            else:
                total[part, mine[first], o2] = block

    for part, (first, second) in enumerate(PARTS):
        block = total[part, mine[first], mine[second]]
        for j2 in FAR_FIRST:
            slot = in_second.at[part, j2 - 1]
            remote(slot, slot, second_send.at[part, j2 - 1], second_recv.at[part, j2 - 1], sibling).wait_recv()
            block += decode(in_second[part, j2 - 1])
        total[part, mine[first], mine[second]] = block
        coded[part, mine[first], mine[second]] = encode(block)
        for dz in (4, 3, 5, 2, 6, 1, 7):
            z = along("z", dz)
            start(remote(
                coded.at[part, mine[first], mine[second], z], in_z.at[part, dz - 1],
                z_send.at[part, dz - 1], z_recv.at[part, dz - 1], device(z=z)))

    for part, (first, second) in enumerate(PARTS):
        piece = total[part, mine[first], mine[second], mine["z"]]
        for dz in (1, 7, 2, 6, 3, 5, 4):
            slot = in_z.at[part, dz - 1]
            remote(slot, slot, z_send.at[part, dz - 1], z_recv.at[part, dz - 1], sibling).wait_recv()
            piece += decode(in_z[part, dz - 1])
        here = gathered.at[core, part, mine[first], mine[second], mine["z"]]
        here[...] = piece.astype(jnp.bfloat16)
        for dz in (4, 3, 5, 2, 6, 1, 7):
            start(remote(
                here, here, out_z_send.at[part, dz - 1], out_z_recv.at[part, dz - 1],
                device(z=along("z", dz))))

    def spread(part, j2):
        first, second = PARTS[part]
        block = gathered.at[core, part, mine[first], along(second, -j2)]
        for away in FAR_FIRST:
            slot = (away - 1) * 4 + j2
            start(remote(
                block, block, out_first_send.at[part, slot], out_first_recv.at[part, slot],
                device(**{first: along(first, away)})))
        start(remote(block, block, fwd_send.at[part, j2], fwd_recv.at[part, j2], sibling))

    for part, (first, second) in enumerate(PARTS):
        for dz in (1, 7, 2, 6, 3, 5, 4):
            there = gathered.at[core, part, mine[first], mine[second], along("z", -dz)]
            remote(there, there, out_z_send.at[part, dz - 1], out_z_recv.at[part, dz - 1], sibling).wait_recv()
        block = gathered.at[core, part, mine[first], mine[second]]
        for j2 in FAR_FIRST:
            start(remote(
                block, block, out_second_send.at[part, j2 - 1], out_second_recv.at[part, j2 - 1],
                device(**{second: along(second, j2)})))
        spread(part, 0)
    for j2 in (1, 3, 2):
        for part, (first, second) in enumerate(PARTS):
            there = gathered.at[core, part, mine[first], along(second, -j2)]
            remote(
                there, there, out_second_send.at[part, j2 - 1], out_second_recv.at[part, j2 - 1], sibling
            ).wait_recv()
            spread(part, j2)

    for load in loads[NX:]:
        load.wait()
    projected = [None, None]

    def add_chunk(which, part, k):
        ranks = jnp.concatenate(
            [gathered[which, part, k, :, z].reshape(128, 128) for z in range(NZ)], axis=1)
        term = dot(v[:, columns(which, k)], ranks, (1, 1))
        projected[part] = term if projected[part] is None else projected[part] + term

    def from_sibling(part, away):
        first, second = PARTS[part]
        k = along(first, -away)
        for j2 in range(4):
            there = gathered.at[1 - core, part, k, along(second, -j2)]
            slot = away * 4 + j2
            remote(there, there, fwd_send.at[part, slot], fwd_recv.at[part, slot], sibling).wait_recv()
        add_chunk(1 - core, part, k)

    for part, (first, second) in enumerate(PARTS):
        add_chunk(core, part, mine[first])
    for away, done in ((1, 0), (3, 1), (2, 3)):
        for part, (first, second) in enumerate(PARTS):
            k = along(first, -away)
            for j2 in (0, 1, 3, 2):
                there = gathered.at[core, part, k, along(second, -j2)]
                slot = (away - 1) * 4 + j2
                remote(
                    there, there, out_first_send.at[part, slot], out_first_recv.at[part, slot], sibling
                ).wait_recv()
                slot = away * 4 + j2
                start(remote(there, there, fwd_send.at[part, slot], fwd_recv.at[part, slot], sibling))
            add_chunk(core, part, k)
        for part in range(2):
            from_sibling(part, done)
    for part in range(2):
        from_sibling(part, 2)

    projected = jnp.concatenate(projected, axis=1)
    p_ref[...] = projected
    gram_in[0] = dot(projected, projected, (0, 0), HIGHEST)

    copy = remote(gram_in.at[0], gram_in.at[1], gx_send.at[0], gx_recv.at[0], sibling)
    start(copy)
    copy.wait_recv()
    gram_chip[...] = (gram_in[0] + gram_in[1]).reshape(2, NY, NX, 8, 256)

    plane = [(dy, dx) for dy in range(NY) for dx in range(NX) if dy or dx]
    scatter = []
    for n, (dy, dx) in enumerate(plane):
        y, x = along("y", dy), along("x", dx)
        copy = remote(
            gram_chip.at[core, y, x], gram_parts.at[n], gx_send.at[1 + n], gx_recv.at[1 + n], device(y=y, x=x))
        copy.start()
        scatter.append(copy)
    sends += scatter
    row = gram_chip[core, mine["y"], mine["x"]]
    for n, copy in enumerate(scatter):
        copy.wait_recv()
        row += gram_parts[n]
    gram_z[mine["z"]] = row
    spread = []
    for dz in range(1, NZ):
        slot = 16 + dz
        z = along("z", dz)
        copy = remote(
            gram_z.at[mine["z"]], gram_z.at[mine["z"]], gx_send.at[slot], gx_recv.at[slot], device(z=z))
        start(copy)
    for dz in range(1, NZ):
        slot = 16 + dz
        z = along("z", -dz)
        remote(gram_z.at[z], gram_z.at[z], gx_send.at[slot], gx_recv.at[slot], sibling).wait_recv()
    row = gram_z[0]
    for n in range(1, NZ):
        row += gram_z[n]
    gram_row[core, mine["y"], mine["x"]] = row
    for n, (dy, dx) in enumerate(plane):
        slot = 24 + n
        here = gram_row.at[core, mine["y"], mine["x"]]
        copy = remote(
            here, here, gx_send.at[slot], gx_recv.at[slot], device(y=along("y", dy), x=along("x", dx)))
        start(copy)
    for n, (dy, dx) in enumerate(plane):
        slot = 24 + n
        there = gram_row.at[core, along("y", -dy), along("x", -dx)]
        remote(there, there, gx_send.at[slot], gx_recv.at[slot], sibling).wait_recv()
    copy = remote(gram_row.at[core], gram_row.at[core], gx_send.at[40], gx_recv.at[40], sibling)
    start(copy)
    arriving = gram_row.at[1 - core]
    remote(arriving, arriving, gx_send.at[40], gx_recv.at[40], sibling).wait_recv()
    g_ref[...] = gram_row[...].reshape(256, 256)
    for part, (first, second) in enumerate(PARTS):
        for away in FAR_FIRST:
            for j2 in range(4):
                first_copy(part, away, along(second, j2)).wait_send()
    for copy in sends:
        copy.wait_send()


def exchange(velocity, basis_in):
    rows, snaps = velocity.shape
    rank = basis_in.shape[1]
    f32, bf16 = jnp.float32, jnp.bfloat16

    def pair(*shape):
        return [pltpu.SemaphoreType.DMA(shape)] * 2

    return pl.pallas_call(
        exchange_kernel,
        out_shape=(
            jax.ShapeDtypeStruct((rows, rank), f32),
            jax.ShapeDtypeStruct((rank, rank), f32),
        ),
        in_specs=[pl.BlockSpec(memory_space=pl.ANY)] * 2,
        out_specs=[pl.BlockSpec(memory_space=pltpu.VMEM)] * 2,
        scratch_shapes=[
            pltpu.VMEM((rows, snaps), bf16),
            pltpu.VMEM((rows, snaps // 2), bf16),
            pltpu.VMEM((rows, rank), bf16),
            pltpu.VMEM((rows, rank), bf16),
            pltpu.VMEM((2, 4, 4, NZ, PIECE, 128), f32),
            pltpu.VMEM((2, 4, 4, NZ, PIECE, 128), bf16),
            pltpu.VMEM((2, 3, 4, NZ, PIECE, 128), bf16),
            pltpu.VMEM((2, 3, NZ, PIECE, 128), bf16),
            pltpu.VMEM((2, NZ - 1, PIECE, 128), bf16),
            pltpu.VMEM((2, 2, 4, 4, NZ, PIECE, 128), bf16),
            pltpu.VMEM((2, rank, rank), f32),
            pltpu.VMEM((2, NY, NX, 8, rank), f32),
            pltpu.VMEM((NY * NX - 1, 8, rank), f32),
            pltpu.VMEM((NZ, 8, rank), f32),
            pltpu.VMEM((2, NY, NX, 8, rank), f32),
            pltpu.SemaphoreType.DMA((2 * NX + 1,)),
            *pair(NX + 1),
            *pair(2, 12),
            *pair(2, 3),
            *pair(2, NZ - 1),
            *pair(2, NZ - 1),
            *pair(2, 3),
            *pair(2, 12),
            *pair(2, 16),
            *pair(41),
        ],
        compiler_params=pltpu.CompilerParams(
            collective_id=0, has_side_effects=True, vmem_limit_bytes=48 * 2**20
        ),
        cost_estimate=pl.CostEstimate(
            flops=4 * rows * snaps * rank, bytes_accessed=2 * rows * snaps, transcendentals=0
        ),
    )(velocity, basis_in)


def factor_kernel(scale, p_ref, g_ref, out_ref, r_ref, w, state):
    size = g_ref.shape[0]
    row = lax.broadcasted_iota(jnp.int32, (size, size), 0)
    col = lax.broadcasted_iota(jnp.int32, (size, size), 1)
    eye = (row == col).astype(jnp.float32)
    weight = jnp.where(row < col, 1.0, 0.5 * eye)
    gram = g_ref[...]
    diagonal = gram * eye
    unit_row = lax.rsqrt(jnp.sum(diagonal, axis=0, keepdims=True))
    unit_col = lax.rsqrt(jnp.sum(diagonal, axis=1, keepdims=True))
    scaled = gram * unit_row * unit_col

    w[...] = eye
    state[...] = scaled - eye

    def go_on(carry):
        count, norm = carry
        return (norm > 1e-6) & (norm < 1e4) & (count < 12)

    def improve():
        upper = state[...] * weight
        once = dot(w[...], upper, (1, 0), HIGHEST)
        w[...] = w[...] - once + dot(once, upper, (1, 0), HIGHEST)

    def step(carry):
        count, _ = carry
        improve()
        excess = dot(w[...], dot(scaled, w[...], (1, 0), HIGHEST), (0, 0), HIGHEST) - eye
        state[...] = excess
        return count + 1, jnp.sum(excess * excess)

    start = state[...]
    _, norm = lax.while_loop(go_on, step, (0, jnp.sum(start * start)))
    converged = norm <= 1e-6

    @pl.when(converged)
    def _():
        improve()

    @pl.when(jnp.logical_not(converged))
    def _():
        state[...] = scaled
        r_ref[...] = jnp.zeros_like(r_ref)
        lane = lax.broadcasted_iota(jnp.int32, (1, size), 1)

        def eliminate(j, _):
            pivot_row = jnp.where(lane >= j, state[pl.ds(j, 1), :], 0.0)
            pivot = jnp.sum(jnp.where(lane == j, pivot_row, 0.0), axis=1, keepdims=True)
            pivot_row = pivot_row / jnp.sqrt(pivot)
            r_ref[pl.ds(j, 1), :] = pivot_row
            pivot_col = jnp.sum(jnp.broadcast_to(pivot_row, (size, size)) * eye, axis=1, keepdims=True)
            state[...] = state[...] - pivot_col * pivot_row
            return 0

        lax.fori_loop(0, size, eliminate, 0)
        w[...] = jnp.zeros_like(w)

        def substitute(n, _):
            j = size - 1 - n
            line = r_ref[pl.ds(j, 1), :]
            pivot = jnp.sum(jnp.where(lane == j, line, 0.0), axis=1, keepdims=True)
            beyond = jnp.where(lane > j, line, 0.0)
            unit = jnp.where(lane == j, 1.0, 0.0)
            w[pl.ds(j, 1), :] = (unit - dot(beyond, w[...], (1, 0), HIGHEST)) / pivot
            return 0

        lax.fori_loop(0, size, substitute, 0)

    triangle = jnp.where(row <= col, dot(w[...], scaled, (0, 0), HIGHEST), 0.0)
    r_ref[...] = triangle / unit_row / scale
    out_ref[...] = dot(p_ref[...], w[...] * unit_col * scale, (1, 0), HIGHEST)


def factor(projected, gram, scale):
    rank = gram.shape[0]
    return pl.pallas_call(
        functools.partial(factor_kernel, scale),
        out_shape=(
            jax.ShapeDtypeStruct(projected.shape, jnp.float32),
            jax.ShapeDtypeStruct((rank, rank), jnp.float32),
        ),
        scratch_shapes=[pltpu.VMEM((rank, rank), jnp.float32)] * 2,
        compiler_params=pltpu.CompilerParams(vmem_limit_bytes=32 * 2**20),
    )(projected, gram)


def local(velocity, basis_in):
    projected, gram = exchange(velocity, basis_in)
    scale = float(lax.axis_size("rows") * velocity.shape[0]) ** 0.5
    return factor(projected, gram, scale)


def solution(mesh):
    in_specs = (P("rows", None), P("rows", None))
    out_specs = (P("rows", None), P())
    return jax.shard_map(local, mesh=mesh, in_specs=in_specs, out_specs=out_specs, check_vma=False)
```

```python
import functools

import jax
import jax.numpy as jnp
from jax import lax
from jax.experimental import pallas as pl
from jax.experimental.pallas import tpu as pltpu
from jax.sharding import PartitionSpec as P

NY, NX, NZ = 4, 4, 8
SIZE = {"x": NX, "z": NZ, "y": NY}
MESH = pl.DeviceIdType.MESH
HIGHEST = lax.Precision.HIGHEST


PARTS = (("x", "y"), ("y", "x"))
PIECE = 16
BLOCKS = 4
FAR_FIRST = (2, 1, 3)
NEAR_FIRST = (1, 3, 2)
Z_FAR_FIRST = (4, 3, 5, 2, 6, 1, 7)
Z_NEAR_FIRST = Z_FAR_FIRST[::-1]
SCALE = 2.0**17


def dot(a, b, contract, precision=None):
    return lax.dot_general(
        a, b, ((contract[:1], contract[1:]), ((), ())),
        precision=precision, preferred_element_type=jnp.float32,
    )


def encode(value):
    scaled = value * SCALE
    return (scaled * scaled * (scaled * jnp.abs(scaled))).astype(jnp.bfloat16)


def decode(code):
    wide = code.astype(jnp.float32)
    power = jnp.maximum(jnp.abs(wide), 1e-37)
    root = lax.rsqrt(power)
    return wide * root * (lax.rsqrt(power * root) * (1.0 / SCALE))


def exchange_kernel(
    v_hbm, b_hbm, p_ref, g_ref,
    v, v_sib, b, b_sib, total, coded, in_first, in_second, in_z, gathered,
    gram_in, gram_chip, gram_parts, gram_z, gram_row,
    load_sem, sib_send, sib_recv, first_send, first_recv, second_send, second_recv,
    z_send, z_recv, out_z_send, out_z_recv, out_second_send, out_second_recv,
    out_first_send, out_first_recv, fwd_send, fwd_recv, gx_send, gx_recv,
):
    me = lax.axis_index("rows")
    core = me % 2
    mine = {"z": me // 2 % NZ, "x": me // (2 * NZ) % NX, "y": me // (2 * NZ * NX)}

    def device(**moved):
        at = {**mine, "core": core, **moved}
        return (((at["y"] * NX + at["x"]) * NZ + at["z"]) * 2 + at["core"],)

    def along(axis, offset):
        return (mine[axis] + offset + SIZE[axis]) % SIZE[axis]

    sibling = device(core=1 - core)

    def remote(source, target, send, recv, to):
        return pltpu.make_async_remote_copy(
            src_ref=source, dst_ref=target, send_sem=send, recv_sem=recv,
            device_id=to, device_id_type=MESH,
        )

    sends = []

    def start(copy):
        copy.start()
        sends.append(copy)

    half = v_sib.shape[1]
    wide = half // (2 * NX)

    def columns(which_core, group, k):
        return pl.ds(pl.multiple_of(which_core * half + (2 * k + group) * wide, 128), wide)

    order = [(group, along("x", offset)) for group in range(2) for offset in FAR_FIRST + (0,)]
    loads = []
    for group, k in order:
        loads.append(pltpu.make_async_copy(
            v_hbm.at[:, columns(core, group, k)], v.at[:, columns(core, group, k)], load_sem.at[len(loads)]))
    others = pl.ds(pl.multiple_of((1 - core) * half, 128), half)
    loads.append(pltpu.make_async_copy(v_hbm.at[:, others], v.at[:, others], load_sem.at[len(loads)]))
    load_b = pltpu.make_async_copy(b_hbm, b, load_sem.at[len(loads)])
    load_b.start()
    for load in loads:
        load.start()

    partners = [sibling]
    for dy in range(NY):
        for dx in range(NX):
            if dy or dx:
                partners.append(device(y=along("y", dy), x=along("x", dx)))
    for dz in range(1, NZ):
        partners.append(device(z=along("z", dz)))
    barrier = pltpu.get_barrier_semaphore()
    for partner in partners:
        pl.semaphore_signal(barrier, inc=1, device_id=partner, device_id_type=MESH)
    pl.semaphore_wait(barrier, len(partners))

    copy_b = remote(b_hbm, b_sib, sib_send.at[8], sib_recv.at[8], sibling)
    start(copy_b)
    copies_v = []
    for n, (group, k) in enumerate(order):
        copy = remote(
            v_hbm.at[:, columns(1 - core, group, k)], v_sib.at[:, pl.ds(n * wide, wide)],
            sib_send.at[n], sib_recv.at[n], sibling)
        start(copy)
        copies_v.append(copy)

    load_b.wait()
    b_t = b[...].T
    copy_b.wait_recv()
    b_sib_t = b_sib[...].T

    def first_copy(group, part, away):
        first, _ = PARTS[part]
        k = along(first, away)
        return remote(
            coded.at[group, part, k], in_first.at[group, part, away - 1],
            first_send.at[group, part, away - 1], first_recv.at[group, part, away - 1], device(**{first: k}))

    for n, (group, k) in enumerate(order):
        loads[n].wait()
        copies_v[n].wait_recv()
        product = dot(b_t, v[:, columns(core, group, k)], (1, 0))
        product += dot(b_sib_t, v_sib[:, n * wide:(n + 1) * wide], (1, 0))
        for part in range(2):
            for z in range(NZ):
                for o2 in range(4):
                    rank = part * 128 + z % 2 * 64 + o2 * PIECE
                    tile = product[rank:rank + PIECE, z // 2 * 128:(z // 2 + 1) * 128]
                    total[group, part, k, o2, z] = tile
                    coded[group, part, k, o2, z] = encode(tile)
        if n % 4 < 3:
            first_copy(group, 0, FAR_FIRST[n % 4]).start()
        away = (k - mine["y"] + NY) % NY

        @pl.when(away != 0)
        def _():
            first_copy(group, 1, away).start()

    def sum_first(group):
        for part, (first, second) in enumerate(PARTS):
            for away in FAR_FIRST:
                first_copy(group, part, away).wait_recv()
            for j2 in FAR_FIRST + (0,):
                o2 = along(second, j2)
                block = total[group, part, mine[first], o2]
                for away in FAR_FIRST:
                    block += decode(in_first[group, part, away - 1, o2])
                if j2:
                    coded[group, part, mine[first], o2] = encode(block)
                    start(remote(
                        coded.at[group, part, mine[first], o2], in_second.at[group, part, j2 - 1],
                        second_send.at[group, part, j2 - 1], second_recv.at[group, part, j2 - 1],
                        device(**{second: o2})))
                else:
                    total[group, part, mine[first], o2] = block

    def sum_second(group):
        for part, (first, second) in enumerate(PARTS):
            at = (group, part, mine[first], mine[second])
            block = total[at]
            for j2 in FAR_FIRST:
                slot = in_second.at[group, part, j2 - 1]
                remote(
                    slot, slot, second_send.at[group, part, j2 - 1], second_recv.at[group, part, j2 - 1], sibling
                ).wait_recv()
                block += decode(in_second[group, part, j2 - 1])
            total[at] = block
            coded[at] = encode(block)
            for dz in Z_FAR_FIRST:
                z = along("z", dz)
                start(remote(
                    coded.at[at + (z,)], in_z.at[group, part, dz - 1],
                    z_send.at[group, part, dz - 1], z_recv.at[group, part, dz - 1], device(z=z)))

    def spread_z(group):
        for part, (first, second) in enumerate(PARTS):
            piece = total[group, part, mine[first], mine[second], mine["z"]]
            for dz in Z_NEAR_FIRST:
                slot = in_z.at[group, part, dz - 1]
                remote(
                    slot, slot, z_send.at[group, part, dz - 1], z_recv.at[group, part, dz - 1], sibling
                ).wait_recv()
                piece += decode(in_z[group, part, dz - 1])
            here = gathered.at[core, group, part, mine[first], mine[second], mine["z"]]
            here[...] = piece.astype(jnp.bfloat16)
            for dz in Z_FAR_FIRST:
                start(remote(
                    here, here, out_z_send.at[group, part, dz - 1], out_z_recv.at[group, part, dz - 1],
                    device(z=along("z", dz))))

    def spread_second(group):
        for part, (first, second) in enumerate(PARTS):
            for dz in Z_NEAR_FIRST:
                there = gathered.at[core, group, part, mine[first], mine[second], along("z", -dz)]
                remote(
                    there, there, out_z_send.at[group, part, dz - 1], out_z_recv.at[group, part, dz - 1], sibling
                ).wait_recv()
            block = gathered.at[core, group, part, mine[first], mine[second]]
            for j2 in FAR_FIRST:
                start(remote(
                    block, block, out_second_send.at[group, part, j2 - 1],
                    out_second_recv.at[group, part, j2 - 1], device(**{second: along(second, j2)})))

    def forward(group, part, away):
        block = gathered.at[core, group, part, along(PARTS[part][0], -away)]
        start(remote(
            block, block, fwd_send.at[group, part, away], fwd_recv.at[group, part, away], sibling))

    def spread_first(group):
        for part, (first, second) in enumerate(PARTS):
            for j2 in NEAR_FIRST:
                there = gathered.at[core, group, part, mine[first], along(second, -j2)]
                remote(
                    there, there, out_second_send.at[group, part, j2 - 1],
                    out_second_recv.at[group, part, j2 - 1], sibling
                ).wait_recv()
            block = gathered.at[core, group, part, mine[first]]
            for away in FAR_FIRST:
                start(remote(
                    block, block, out_first_send.at[group, part, away - 1],
                    out_first_recv.at[group, part, away - 1], device(**{first: along(first, away)})))
            forward(group, part, 0)

    def add_chunk(which, group, part, away):
        k = along(PARTS[part][0], -away)
        ranks = jnp.concatenate([
            jnp.concatenate([
                gathered[which, group, part, k, :, 2 * n + h].reshape(4 * PIECE, 128) for h in range(2)
            ], axis=0)
            for n in range(BLOCKS)
        ], axis=1)
        term = dot(v[:, columns(which, group, k)], ranks, (1, 1))
        p_ref[:, part * 128:(part + 1) * 128] += term

    def from_chip(group, away):
        for part, (first, second) in enumerate(PARTS):
            if away:
                there = gathered.at[core, group, part, along(first, -away)]
                remote(
                    there, there, out_first_send.at[group, part, away - 1],
                    out_first_recv.at[group, part, away - 1], sibling
                ).wait_recv()
                forward(group, part, away)
        for part in range(2):
            add_chunk(core, group, part, away)

    def from_sibling(group, away):
        for part, (first, second) in enumerate(PARTS):
            there = gathered.at[1 - core, group, part, along(first, -away)]
            remote(
                there, there, fwd_send.at[group, part, away], fwd_recv.at[group, part, away], sibling
            ).wait_recv()
            add_chunk(1 - core, group, part, away)

    sum_first(0)
    sum_second(0)
    sum_first(1)
    spread_z(0)
    sum_second(1)
    spread_second(0)
    spread_z(1)
    spread_first(0)
    p_ref[...] = jnp.zeros_like(p_ref)
    loads[8].wait()
    from_chip(0, 0)
    spread_second(1)
    from_chip(0, 1)
    from_sibling(0, 0)
    spread_first(1)
    from_chip(0, 3)
    from_chip(1, 0)
    from_sibling(0, 1)
    from_chip(0, 2)
    from_sibling(0, 3)
    from_sibling(1, 0)
    from_chip(1, 1)
    from_sibling(0, 2)
    from_chip(1, 3)
    from_sibling(1, 1)
    from_chip(1, 2)
    from_sibling(1, 3)
    from_sibling(1, 2)

    projected = p_ref[...]
    gram_in[0] = dot(projected, projected, (0, 0), HIGHEST)

    copy = remote(gram_in.at[0], gram_in.at[1], gx_send.at[0], gx_recv.at[0], sibling)
    start(copy)
    copy.wait_recv()
    gram_chip[...] = (gram_in[0] + gram_in[1]).reshape(NY, NX, 16, 256)

    plane = [(dy, dx) for dy in (2, 1, 3, 0) for dx in (2, 1, 3, 0) if dy or dx]
    scatter = []
    for n, (dy, dx) in enumerate(plane):
        y, x = along("y", dy), along("x", dx)
        copy = remote(
            gram_chip.at[y, x], gram_parts.at[n], gx_send.at[1 + n], gx_recv.at[1 + n], device(y=y, x=x))
        start(copy)
        scatter.append(copy)
    row = gram_chip[mine["y"], mine["x"]]
    for n, copy in reversed(list(enumerate(scatter))):
        copy.wait_recv()
        row += gram_parts[n]
    gram_z[mine["z"]] = row
    for dz in Z_FAR_FIRST:
        slot = 16 + dz
        here = gram_z.at[mine["z"]]
        start(remote(here, here, gx_send.at[slot], gx_recv.at[slot], device(z=along("z", dz))))
    for dz in Z_NEAR_FIRST:
        slot = 16 + dz
        there = gram_z.at[along("z", -dz)]
        remote(there, there, gx_send.at[slot], gx_recv.at[slot], sibling).wait_recv()
    row = gram_z[0]
    for n in range(1, NZ):
        row += gram_z[n]
    gram_row[mine["y"], mine["x"]] = row
    for n, (dy, dx) in enumerate(plane):
        slot = 24 + n
        here = gram_row.at[mine["y"], mine["x"]]
        start(remote(
            here, here, gx_send.at[slot], gx_recv.at[slot], device(y=along("y", dy), x=along("x", dx))))
    for n, (dy, dx) in enumerate(plane):
        slot = 24 + n
        there = gram_row.at[along("y", -dy), along("x", -dx)]
        remote(there, there, gx_send.at[slot], gx_recv.at[slot], sibling).wait_recv()
    g_ref[...] = gram_row[...].reshape(256, 256)
    for group in range(2):
        for part in range(2):
            for away in FAR_FIRST:
                first_copy(group, part, away).wait_send()
    for copy in sends:
        copy.wait_send()


def exchange(velocity, basis_in):
    rows, snaps = velocity.shape
    rank = basis_in.shape[1]
    f32, bf16 = jnp.float32, jnp.bfloat16

    def pair(*shape):
        return [pltpu.SemaphoreType.DMA(shape)] * 2

    return pl.pallas_call(
        exchange_kernel,
        out_shape=(
            jax.ShapeDtypeStruct((rows, rank), f32),
            jax.ShapeDtypeStruct((rank, rank), f32),
        ),
        in_specs=[pl.BlockSpec(memory_space=pltpu.HBM)] * 2,
        out_specs=[pl.BlockSpec(memory_space=pltpu.VMEM)] * 2,
        scratch_shapes=[
            pltpu.VMEM((rows, snaps), bf16),
            pltpu.VMEM((rows, snaps // 2), bf16),
            pltpu.VMEM((rows, rank), bf16),
            pltpu.VMEM((rows, rank), bf16),
            pltpu.VMEM((2, 2, 4, 4, NZ, PIECE, 128), f32),
            pltpu.VMEM((2, 2, 4, 4, NZ, PIECE, 128), bf16),
            pltpu.VMEM((2, 2, 3, 4, NZ, PIECE, 128), bf16),
            pltpu.VMEM((2, 2, 3, NZ, PIECE, 128), bf16),
            pltpu.VMEM((2, 2, NZ - 1, PIECE, 128), bf16),
            pltpu.VMEM((2, 2, 2, 4, 4, NZ, PIECE, 128), bf16),
            pltpu.VMEM((2, rank, rank), f32),
            pltpu.VMEM((NY, NX, 16, rank), f32),
            pltpu.VMEM((NY * NX - 1, 16, rank), f32),
            pltpu.VMEM((NZ, 16, rank), f32),
            pltpu.VMEM((NY, NX, 16, rank), f32),
            pltpu.SemaphoreType.DMA((10,)),
            *pair(9),
            *pair(2, 2, 3),
            *pair(2, 2, 3),
            *pair(2, 2, NZ - 1),
            *pair(2, 2, NZ - 1),
            *pair(2, 2, 3),
            *pair(2, 2, 3),
            *pair(2, 2, 4),
            *pair(39),
        ],
        compiler_params=pltpu.CompilerParams(
            collective_id=0, has_side_effects=True, vmem_limit_bytes=48 * 2**20
        ),
        cost_estimate=pl.CostEstimate(
            flops=4 * rows * snaps * rank, bytes_accessed=2 * rows * snaps, transcendentals=0
        ),
    )(velocity, basis_in)


def factor_kernel(scale, p_ref, g_ref, out_ref, r_ref, w, state):
    size = g_ref.shape[0]
    row = lax.broadcasted_iota(jnp.int32, (size, size), 0)
    col = lax.broadcasted_iota(jnp.int32, (size, size), 1)
    eye = (row == col).astype(jnp.float32)
    weight = jnp.where(row < col, 1.0, 0.5 * eye)
    gram = g_ref[...]
    diagonal = gram * eye
    unit_row = lax.rsqrt(jnp.sum(diagonal, axis=0, keepdims=True))
    unit_col = lax.rsqrt(jnp.sum(diagonal, axis=1, keepdims=True))
    scaled = gram * unit_row * unit_col

    w[...] = eye
    state[...] = scaled - eye

    def go_on(carry):
        count, norm = carry
        return (norm > 1e-6) & (norm < 1e4) & (count < 12)

    def improve():
        upper = state[...] * weight
        once = dot(w[...], upper, (1, 0), HIGHEST)
        w[...] = w[...] - once + dot(once, upper, (1, 0), HIGHEST)

    def step(carry):
        count, _ = carry
        improve()
        excess = dot(w[...], dot(scaled, w[...], (1, 0), HIGHEST), (0, 0), HIGHEST) - eye
        state[...] = excess
        return count + 1, jnp.sum(excess * excess)

    start = state[...]
    _, norm = lax.while_loop(go_on, step, (0, jnp.sum(start * start)))
    converged = norm <= 1e-6

    @pl.when(converged)
    def _():
        improve()

    @pl.when(jnp.logical_not(converged))
    def _():
        state[...] = scaled
        r_ref[...] = jnp.zeros_like(r_ref)
        lane = lax.broadcasted_iota(jnp.int32, (1, size), 1)

        def eliminate(j, _):
            pivot_row = jnp.where(lane >= j, state[pl.ds(j, 1), :], 0.0)
            pivot = jnp.sum(jnp.where(lane == j, pivot_row, 0.0), axis=1, keepdims=True)
            pivot_row = pivot_row / jnp.sqrt(pivot)
            r_ref[pl.ds(j, 1), :] = pivot_row
            pivot_col = jnp.sum(jnp.broadcast_to(pivot_row, (size, size)) * eye, axis=1, keepdims=True)
            state[...] = state[...] - pivot_col * pivot_row
            return 0

        lax.fori_loop(0, size, eliminate, 0)
        w[...] = jnp.zeros_like(w)

        def substitute(n, _):
            j = size - 1 - n
            line = r_ref[pl.ds(j, 1), :]
            pivot = jnp.sum(jnp.where(lane == j, line, 0.0), axis=1, keepdims=True)
            beyond = jnp.where(lane > j, line, 0.0)
            unit = jnp.where(lane == j, 1.0, 0.0)
            w[pl.ds(j, 1), :] = (unit - dot(beyond, w[...], (1, 0), HIGHEST)) / pivot
            return 0

        lax.fori_loop(0, size, substitute, 0)

    triangle = jnp.where(row <= col, dot(w[...], scaled, (0, 0), HIGHEST), 0.0)
    r_ref[...] = triangle / unit_row / scale
    out_ref[...] = dot(p_ref[...], w[...] * unit_col * scale, (1, 0), HIGHEST)


def factor(projected, gram, scale):
    rank = gram.shape[0]
    return pl.pallas_call(
        functools.partial(factor_kernel, scale),
        out_shape=(
            jax.ShapeDtypeStruct(projected.shape, jnp.float32),
            jax.ShapeDtypeStruct((rank, rank), jnp.float32),
        ),
        scratch_shapes=[pltpu.VMEM((rank, rank), jnp.float32)] * 2,
        compiler_params=pltpu.CompilerParams(vmem_limit_bytes=32 * 2**20),
    )(projected, gram)


def local(velocity, basis_in):
    projected, gram = exchange(velocity, basis_in)
    scale = float(lax.axis_size("rows") * velocity.shape[0]) ** 0.5
    return factor(projected, gram, scale)


def solution(mesh):
    in_specs = (P("rows", None), P("rows", None))
    out_specs = (P("rows", None), P())
    return jax.shard_map(local, mesh=mesh, in_specs=in_specs, out_specs=out_specs, check_vma=False)
```

```python
import functools

import jax
import jax.numpy as jnp
from jax import lax
from jax.experimental import pallas as pl
from jax.experimental.pallas import tpu as pltpu
from jax.sharding import PartitionSpec as P

NY, NX, NZ = 4, 4, 8
SIZE = {"x": NX, "z": NZ, "y": NY}
MESH = pl.DeviceIdType.MESH
HIGHEST = lax.Precision.HIGHEST


PARTS = (("x", "y"), ("y", "x"))
PIECE = 16
BLOCKS = 4
FAR_FIRST = (2, 1, 3)
NEAR_FIRST = (1, 3, 2)
Z_FAR_FIRST = (4, 3, 5, 2, 6, 1, 7)
Z_NEAR_FIRST = Z_FAR_FIRST[::-1]
SCALE = 2.0**17


def dot(a, b, contract, precision=None):
    return lax.dot_general(
        a, b, ((contract[:1], contract[1:]), ((), ())),
        precision=precision, preferred_element_type=jnp.float32,
    )


def encode(value):
    scaled = value * SCALE
    return (scaled * scaled * (scaled * jnp.abs(scaled))).astype(jnp.bfloat16)


def decode(code):
    wide = code.astype(jnp.float32)
    power = jnp.maximum(jnp.abs(wide), 1e-37)
    root = lax.rsqrt(power)
    return wide * root * (lax.rsqrt(power * root) * (1.0 / SCALE))


def exchange_kernel(
    v_hbm, b_hbm, p_hbm, g_ref,
    p_ref, v, v_sib, b, b_sib, early, total, coded, in_far, in_near, in_second, in_z, gathered,
    gram_in, gram_chip, gram_parts, gram_z, gram_row,
    load_sem, sib_send, sib_recv, far_send, far_recv, near_send, near_recv, second_send, second_recv,
    z_send, z_recv, out_z_send, out_z_recv, out_second_send, out_second_recv,
    out_first_send, out_first_recv, fwd_send, fwd_recv, gx_send, gx_recv,
):
    me = lax.axis_index("rows")
    core = me % 2
    mine = {"z": me // 2 % NZ, "x": me // (2 * NZ) % NX, "y": me // (2 * NZ * NX)}

    def device(**moved):
        at = {**mine, "core": core, **moved}
        return (((at["y"] * NX + at["x"]) * NZ + at["z"]) * 2 + at["core"],)

    def along(axis, offset):
        return (mine[axis] + offset + SIZE[axis]) % SIZE[axis]

    sibling = device(core=1 - core)

    def remote(source, target, send, recv, to):
        return pltpu.make_async_remote_copy(
            src_ref=source, dst_ref=target, send_sem=send, recv_sem=recv,
            device_id=to, device_id_type=MESH,
        )

    sends = []

    def start(copy):
        copy.start()
        sends.append(copy)

    half = v_sib.shape[1]
    wide = half // (2 * NX)

    def columns(which_core, group, k):
        return pl.ds(pl.multiple_of(which_core * half + (2 * k + group) * wide, 128), wide)

    apart = (mine["y"] - mine["x"] + 4) % 4
    same, three = 1 - (apart + 3) // 4, apart % 2 * (apart // 2)
    one, two = apart % 2 * (1 - apart // 2), (1 - apart % 2) * (apart // 2)
    offsets = (2, same + 3 * one + three, 3 * same + one + two + 3 * three, 3 * two)
    order = [(group, along("x", offset)) for group in range(2) for offset in offsets]
    loads = []
    for group, k in order:
        loads.append(pltpu.make_async_copy(
            v_hbm.at[:, columns(core, group, k)], v.at[:, columns(core, group, k)], load_sem.at[len(loads)]))
    others = pl.ds(pl.multiple_of((1 - core) * half, 128), half)
    loads.append(pltpu.make_async_copy(v_hbm.at[:, others], v.at[:, others], load_sem.at[len(loads)]))
    load_b = pltpu.make_async_copy(b_hbm, b, load_sem.at[len(loads)])
    load_b.start()
    for load in loads:
        load.start()

    partners = [sibling]
    for dy in range(NY):
        for dx in range(NX):
            if dy or dx:
                partners.append(device(y=along("y", dy), x=along("x", dx)))
    for dz in range(1, NZ):
        partners.append(device(z=along("z", dz)))
    barrier = pltpu.get_barrier_semaphore()
    for partner in partners:
        pl.semaphore_signal(barrier, inc=1, device_id=partner, device_id_type=MESH)

    load_b.wait()
    b_t = b[...].T
    for n in range(4):
        loads[n].wait()
        early[n] = dot(b_t, v[:, columns(core, *order[n])], (1, 0))
    pl.semaphore_wait(barrier, len(partners))

    copy_b = remote(b_hbm, b_sib, sib_send.at[8], sib_recv.at[8], sibling)
    start(copy_b)
    copies_v = []
    for n, (group, k) in enumerate(order):
        copy = remote(
            v_hbm.at[:, columns(1 - core, group, k)], v_sib.at[:, pl.ds(n * wide, wide)],
            sib_send.at[n], sib_recv.at[n], sibling)
        start(copy)
        copies_v.append(copy)

    copy_b.wait_recv()
    b_sib_t = b_sib[...].T

    def far_copy(group, part, way):
        first, _ = PARTS[part]
        return remote(
            coded.at[group, part, along(first, 2), pl.ds(2 * way, 2)], in_far.at[group, part, way],
            far_send.at[group, part, way], far_recv.at[group, part, way],
            device(**{first: along(first, 1 - 2 * way)}))

    def near_copy(group, part, way, relay):
        first, _ = PARTS[part]
        k = along(first, 1 - 2 * way)
        half_of = pl.ds(2 * way if relay else 2 - 2 * way, 2)
        slot = 2 * way + relay
        return remote(
            coded.at[group, part, k, half_of], in_near.at[group, part, way, half_of],
            near_send.at[group, part, slot], near_recv.at[group, part, slot], device(**{first: k}))

    def relay(group):
        for part, (first, _) in enumerate(PARTS):
            for way in range(2):
                far_copy(group, part, way).wait_recv()
                at = (group, part, along(first, 1 - 2 * way), pl.ds(2 * way, 2))
                coded[at] = encode(total[at] + decode(in_far[group, part, way]))
                near_copy(group, part, way, 1).start()

    for n, (group, k) in enumerate(order):
        if group:
            loads[n].wait()
            product = dot(b_t, v[:, columns(core, group, k)], (1, 0))
        else:
            product = early[n]
        copies_v[n].wait_recv()
        product += dot(b_sib_t, v_sib[:, n * wide:(n + 1) * wide], (1, 0))
        for part in range(2):
            for z in range(NZ):
                for o2 in range(4):
                    rank = part * 128 + z % 2 * 64 + o2 * PIECE
                    tile = product[rank:rank + PIECE, z // 2 * 128:(z // 2 + 1) * 128]
                    total[group, part, k, o2, z] = tile
                    coded[group, part, k, o2, z] = encode(tile)
        for part, (first, _) in enumerate(PARTS):
            away = (k - mine[first] + 4) % 4

            @pl.when(away == 2)
            def _():
                for way in range(2):
                    far_copy(group, part, way).start()

            @pl.when(away % 2 == 1)
            def _():
                near_copy(group, part, away // 2, 0).start()
        if n == 5:
            relay(0)
    relay(1)

    def sum_first(group):
        for part, (first, second) in enumerate(PARTS):
            for way in range(2):
                for kind in range(2):
                    near_copy(group, part, way, kind).wait_recv()
            for j2 in FAR_FIRST + (0,):
                o2 = along(second, j2)
                block = total[group, part, mine[first], o2]
                for way in range(2):
                    block += decode(in_near[group, part, way, o2])
                if j2:
                    coded[group, part, mine[first], o2] = encode(block)
                    start(remote(
                        coded.at[group, part, mine[first], o2], in_second.at[group, part, j2 - 1],
                        second_send.at[group, part, j2 - 1], second_recv.at[group, part, j2 - 1],
                        device(**{second: o2})))
                else:
                    total[group, part, mine[first], o2] = block

    def sum_second(group):
        for part, (first, second) in enumerate(PARTS):
            at = (group, part, mine[first], mine[second])
            block = total[at]
            for j2 in FAR_FIRST:
                slot = in_second.at[group, part, j2 - 1]
                remote(
                    slot, slot, second_send.at[group, part, j2 - 1], second_recv.at[group, part, j2 - 1], sibling
                ).wait_recv()
                block += decode(in_second[group, part, j2 - 1])
            total[at] = block
            coded[at] = encode(block)
            for dz in Z_FAR_FIRST:
                z = along("z", dz)
                start(remote(
                    coded.at[at + (z,)], in_z.at[group, part, dz - 1],
                    z_send.at[group, part, dz - 1], z_recv.at[group, part, dz - 1], device(z=z)))

    def spread_z(group):
        for part, (first, second) in enumerate(PARTS):
            piece = total[group, part, mine[first], mine[second], mine["z"]]
            for dz in Z_NEAR_FIRST:
                slot = in_z.at[group, part, dz - 1]
                remote(
                    slot, slot, z_send.at[group, part, dz - 1], z_recv.at[group, part, dz - 1], sibling
                ).wait_recv()
                piece += decode(in_z[group, part, dz - 1])
            here = gathered.at[core, group, part, mine[first], mine[second], mine["z"]]
            here[...] = piece.astype(jnp.bfloat16)
            for dz in Z_FAR_FIRST:
                start(remote(
                    here, here, out_z_send.at[group, part, dz - 1], out_z_recv.at[group, part, dz - 1],
                    device(z=along("z", dz))))

    def spread_second(group):
        for part, (first, second) in enumerate(PARTS):
            for dz in Z_NEAR_FIRST:
                there = gathered.at[core, group, part, mine[first], mine[second], along("z", -dz)]
                remote(
                    there, there, out_z_send.at[group, part, dz - 1], out_z_recv.at[group, part, dz - 1], sibling
                ).wait_recv()
            block = gathered.at[core, group, part, mine[first], mine[second]]
            for j2 in FAR_FIRST:
                start(remote(
                    block, block, out_second_send.at[group, part, j2 - 1],
                    out_second_recv.at[group, part, j2 - 1], device(**{second: along(second, j2)})))

    def forward(group, part, away):
        block = gathered.at[core, group, part, along(PARTS[part][0], -away)]
        start(remote(
            block, block, fwd_send.at[group, part, away], fwd_recv.at[group, part, away], sibling))

    def spread_first(group):
        for part, (first, second) in enumerate(PARTS):
            for j2 in NEAR_FIRST:
                there = gathered.at[core, group, part, mine[first], along(second, -j2)]
                remote(
                    there, there, out_second_send.at[group, part, j2 - 1],
                    out_second_recv.at[group, part, j2 - 1], sibling
                ).wait_recv()
            block = gathered.at[core, group, part, mine[first]]
            for away in FAR_FIRST:
                start(remote(
                    block, block, out_first_send.at[group, part, away - 1],
                    out_first_recv.at[group, part, away - 1], device(**{first: along(first, away)})))
            forward(group, part, 0)

    def add_chunk(which, group, part, away):
        k = along(PARTS[part][0], -away)
        ranks = jnp.concatenate([
            jnp.concatenate([
                gathered[which, group, part, k, :, 2 * n + h].reshape(4 * PIECE, 128) for h in range(2)
            ], axis=0)
            for n in range(BLOCKS)
        ], axis=1)
        term = dot(v[:, columns(which, group, k)], ranks, (1, 1))
        p_ref[:, part * 128:(part + 1) * 128] += term

    def from_chip(group, away):
        for part, (first, second) in enumerate(PARTS):
            if away:
                there = gathered.at[core, group, part, along(first, -away)]
                remote(
                    there, there, out_first_send.at[group, part, away - 1],
                    out_first_recv.at[group, part, away - 1], sibling
                ).wait_recv()
                forward(group, part, away)
        for part in range(2):
            add_chunk(core, group, part, away)

    def from_sibling(group, away):
        for part, (first, second) in enumerate(PARTS):
            there = gathered.at[1 - core, group, part, along(first, -away)]
            remote(
                there, there, fwd_send.at[group, part, away], fwd_recv.at[group, part, away], sibling
            ).wait_recv()
            add_chunk(1 - core, group, part, away)

    sum_first(0)
    sum_second(0)
    sum_first(1)
    spread_z(0)
    sum_second(1)
    spread_second(0)
    spread_z(1)
    spread_first(0)
    p_ref[...] = jnp.zeros_like(p_ref)
    loads[8].wait()
    from_chip(0, 0)
    spread_second(1)
    from_chip(0, 1)
    from_sibling(0, 0)
    spread_first(1)
    from_chip(0, 3)
    from_chip(1, 0)
    from_sibling(0, 1)
    from_chip(0, 2)
    from_sibling(0, 3)
    from_sibling(1, 0)
    from_chip(1, 1)
    from_sibling(0, 2)
    from_chip(1, 3)
    from_sibling(1, 1)
    from_chip(1, 2)
    from_sibling(1, 3)
    from_sibling(1, 2)

    projected = p_ref[...]
    store = pltpu.make_async_copy(p_ref, p_hbm, load_sem.at[10])
    store.start()
    gram_in[0] = dot(projected, projected, (0, 0), HIGHEST)

    copy = remote(gram_in.at[0], gram_in.at[1], gx_send.at[0], gx_recv.at[0], sibling)
    start(copy)
    copy.wait_recv()
    gram_chip[...] = (gram_in[0] + gram_in[1]).reshape(NY, NX, 16, 256)

    plane = [(dy, dx) for dy in (2, 1, 3, 0) for dx in (2, 1, 3, 0) if dy or dx]
    scatter = []
    for n, (dy, dx) in enumerate(plane):
        y, x = along("y", dy), along("x", dx)
        copy = remote(
            gram_chip.at[y, x], gram_parts.at[n], gx_send.at[1 + n], gx_recv.at[1 + n], device(y=y, x=x))
        start(copy)
        scatter.append(copy)
    row = gram_chip[mine["y"], mine["x"]]
    for n, copy in reversed(list(enumerate(scatter))):
        copy.wait_recv()
        row += gram_parts[n]
    gram_z[mine["z"]] = row
    for dz in Z_FAR_FIRST:
        slot = 16 + dz
        here = gram_z.at[mine["z"]]
        start(remote(here, here, gx_send.at[slot], gx_recv.at[slot], device(z=along("z", dz))))
    for dz in Z_NEAR_FIRST:
        slot = 16 + dz
        there = gram_z.at[along("z", -dz)]
        remote(there, there, gx_send.at[slot], gx_recv.at[slot], sibling).wait_recv()
    row = gram_z[0]
    for n in range(1, NZ):
        row += gram_z[n]
    gram_row[mine["y"], mine["x"]] = row
    for n, (dy, dx) in enumerate(plane):
        slot = 24 + n
        here = gram_row.at[mine["y"], mine["x"]]
        start(remote(
            here, here, gx_send.at[slot], gx_recv.at[slot], device(y=along("y", dy), x=along("x", dx))))
    for n, (dy, dx) in enumerate(plane):
        slot = 24 + n
        there = gram_row.at[along("y", -dy), along("x", -dx)]
        remote(there, there, gx_send.at[slot], gx_recv.at[slot], sibling).wait_recv()
    g_ref[...] = gram_row[...].reshape(256, 256)
    store.wait()
    for group in range(2):
        for part in range(2):
            for way in range(2):
                far_copy(group, part, way).wait_send()
                for kind in range(2):
                    near_copy(group, part, way, kind).wait_send()
    for copy in sends:
        copy.wait_send()


def exchange(velocity, basis_in):
    rows, snaps = velocity.shape
    rank = basis_in.shape[1]
    f32, bf16 = jnp.float32, jnp.bfloat16

    def pair(*shape):
        return [pltpu.SemaphoreType.DMA(shape)] * 2

    return pl.pallas_call(
        exchange_kernel,
        out_shape=(
            jax.ShapeDtypeStruct((rows, rank), f32),
            jax.ShapeDtypeStruct((rank, rank), f32),
        ),
        in_specs=[pl.BlockSpec(memory_space=pltpu.HBM)] * 2,
        out_specs=[pl.BlockSpec(memory_space=pl.ANY), pl.BlockSpec(memory_space=pltpu.VMEM)],
        scratch_shapes=[
            pltpu.VMEM((rows, rank), f32),
            pltpu.VMEM((rows, snaps), bf16),
            pltpu.VMEM((rows, snaps // 2), bf16),
            pltpu.VMEM((rows, rank), bf16),
            pltpu.VMEM((rows, rank), bf16),
            pltpu.VMEM((4, rank, snaps // 16), f32),
            pltpu.VMEM((2, 2, 4, 4, NZ, PIECE, 128), f32),
            pltpu.VMEM((2, 2, 4, 4, NZ, PIECE, 128), bf16),
            pltpu.VMEM((2, 2, 2, 2, NZ, PIECE, 128), bf16),
            pltpu.VMEM((2, 2, 2, 4, NZ, PIECE, 128), bf16),
            pltpu.VMEM((2, 2, 3, NZ, PIECE, 128), bf16),
            pltpu.VMEM((2, 2, NZ - 1, PIECE, 128), bf16),
            pltpu.VMEM((2, 2, 2, 4, 4, NZ, PIECE, 128), bf16),
            pltpu.VMEM((2, rank, rank), f32),
            pltpu.VMEM((NY, NX, 16, rank), f32),
            pltpu.VMEM((NY * NX - 1, 16, rank), f32),
            pltpu.VMEM((NZ, 16, rank), f32),
            pltpu.VMEM((NY, NX, 16, rank), f32),
            pltpu.SemaphoreType.DMA((11,)),
            *pair(9),
            *pair(2, 2, 2),
            *pair(2, 2, 4),
            *pair(2, 2, 3),
            *pair(2, 2, NZ - 1),
            *pair(2, 2, NZ - 1),
            *pair(2, 2, 3),
            *pair(2, 2, 3),
            *pair(2, 2, 4),
            *pair(39),
        ],
        compiler_params=pltpu.CompilerParams(
            collective_id=0, has_side_effects=True, vmem_limit_bytes=107 * 2**19
        ),
        cost_estimate=pl.CostEstimate(
            flops=4 * rows * snaps * rank, bytes_accessed=2 * rows * snaps, transcendentals=0
        ),
    )(velocity, basis_in)


def split_dot(a, b):
    a_high, b_high = a.astype(jnp.bfloat16), b.astype(jnp.bfloat16)
    a_low = (a - a_high.astype(jnp.float32)).astype(jnp.bfloat16)
    b_low = (b - b_high.astype(jnp.float32)).astype(jnp.bfloat16)
    return dot(a_high, b_high, (1, 0)) + (dot(a_high, b_low, (1, 0)) + dot(a_low, b_high, (1, 0)))


def factor_kernel(scale, p_hbm, g_ref, out_hbm, r_hbm, p_ref, out, r_ref, moved, state, sem):
    load = pltpu.make_async_copy(p_hbm, p_ref, sem.at[5])
    load.start()
    size = g_ref.shape[0]
    bf16 = jnp.bfloat16
    row = lax.broadcasted_iota(jnp.int32, (size, size), 0)
    col = lax.broadcasted_iota(jnp.int32, (size, size), 1)
    eye = (row == col).astype(jnp.float32)
    weight = jnp.where(row < col, 1.0, 0.5 * eye)
    gram = g_ref[...]
    diagonal = gram * eye
    unit_row = lax.rsqrt(jnp.sum(diagonal, axis=0, keepdims=True))
    unit_col = lax.rsqrt(jnp.sum(diagonal, axis=1, keepdims=True))
    scaled = gram * unit_row * unit_col
    excess = scaled - eye

    def refine(u):
        small = u.astype(bf16)
        return u - weight * dot(small, small, (0, 0))

    def advance(d, u, exact):
        x = refine(u) if exact else u
        small = x.astype(bf16)
        y = x - dot(small, small, (1, 0))
        if exact:
            return d - y - dot(d, y, (1, 0), HIGHEST)
        return d - y - dot(d.astype(bf16), y.astype(bf16), (1, 0))

    def rest(d, exact):
        if exact:
            once = excess + dot(excess, d, (1, 0), HIGHEST)
            return weight * (once + dot(d, d + once, (0, 0), HIGHEST)) + d
        near = d.astype(bf16)
        once = excess + dot(excess.astype(bf16), near, (1, 0))
        return weight * (once + dot(near, (d + once).astype(bf16), (0, 0))) + d

    x = refine(weight * excess)
    small = x.astype(bf16)
    square = dot(small, small, (1, 0))
    d = square - x - dot(square.astype(bf16), small, (1, 0))
    d = advance(d, rest(d, False), False)
    u = rest(d, True)
    moved[...] = d
    state[...] = u

    def go_on(carry):
        count, norm = carry
        return (norm > 2e-5) & (norm < 1e4) & (count < 12)

    def step(carry):
        count, _ = carry
        d = advance(moved[...], state[...], True)
        u = rest(d, True)
        moved[...] = d
        state[...] = u
        return count + 1, jnp.sum(u * u)

    _, norm = lax.while_loop(go_on, step, (0, jnp.sum(u * u)))
    converged = norm <= 2e-5

    @pl.when(converged)
    def _():
        moved[...] = advance(moved[...], state[...], True)

    @pl.when(jnp.logical_not(converged))
    def _():
        state[...] = scaled
        r_ref[...] = jnp.zeros_like(r_ref)
        lane = lax.broadcasted_iota(jnp.int32, (1, size), 1)

        def eliminate(j, _):
            pivot_row = jnp.where(lane >= j, state[pl.ds(j, 1), :], 0.0)
            pivot = jnp.sum(jnp.where(lane == j, pivot_row, 0.0), axis=1, keepdims=True)
            pivot_row = pivot_row / jnp.sqrt(pivot)
            r_ref[pl.ds(j, 1), :] = pivot_row
            pivot_col = jnp.sum(jnp.broadcast_to(pivot_row, (size, size)) * eye, axis=1, keepdims=True)
            state[...] = state[...] - pivot_col * pivot_row
            return 0

        lax.fori_loop(0, size, eliminate, 0)
        moved[...] = jnp.zeros_like(moved)

        def substitute(n, _):
            j = size - 1 - n
            line = r_ref[pl.ds(j, 1), :]
            pivot = jnp.sum(jnp.where(lane == j, line, 0.0), axis=1, keepdims=True)
            beyond = jnp.where(lane > j, line, 0.0)
            unit = jnp.where(lane == j, 1.0, 0.0)
            moved[pl.ds(j, 1), :] = (unit - dot(beyond, moved[...], (1, 0), HIGHEST)) / pivot
            return 0

        lax.fori_loop(0, size, substitute, 0)
        moved[...] = moved[...] - eye

    d = moved[...]
    load.wait()
    copies = []
    rows = p_ref.shape[0] // 4
    for n in range(4):
        block = pl.ds(n * rows, rows)
        p = p_ref[block, :] * (unit_row * scale)
        out[block, :] = p + split_dot(p, d)
        copy = pltpu.make_async_copy(out.at[block, :], out_hbm.at[block, :], sem.at[n])
        copy.start()
        copies.append(copy)
    triangle = jnp.where(row <= col, scaled + dot(d, scaled, (0, 0), HIGHEST), 0.0)
    r_ref[...] = triangle / (unit_row * scale)
    copy = pltpu.make_async_copy(r_ref, r_hbm, sem.at[4])
    copy.start()
    copies.append(copy)
    for copy in copies:
        copy.wait()


def factor(projected, gram, scale):
    rank = gram.shape[0]
    return pl.pallas_call(
        functools.partial(factor_kernel, scale),
        out_shape=(
            jax.ShapeDtypeStruct(projected.shape, jnp.float32),
            jax.ShapeDtypeStruct((rank, rank), jnp.float32),
        ),
        in_specs=[pl.BlockSpec(memory_space=pl.ANY), pl.BlockSpec(memory_space=pltpu.VMEM)],
        out_specs=[pl.BlockSpec(memory_space=pl.ANY)] * 2,
        scratch_shapes=[
            *[pltpu.VMEM(projected.shape, jnp.float32)] * 2,
            *[pltpu.VMEM((rank, rank), jnp.float32)] * 3,
            pltpu.SemaphoreType.DMA((6,)),
        ],
        compiler_params=pltpu.CompilerParams(vmem_limit_bytes=107 * 2**19),
    )(projected, gram)


def local(velocity, basis_in):
    projected, gram = exchange(velocity, basis_in)
    scale = float(lax.axis_size("rows") * velocity.shape[0]) ** 0.5
    return factor(projected, gram, scale)


def solution(mesh):
    in_specs = (P("rows", None), P("rows", None))
    out_specs = (P("rows", None), P())
    return jax.shard_map(local, mesh=mesh, in_specs=in_specs, out_specs=out_specs, check_vma=False)
```

```python
import functools

import jax
import jax.numpy as jnp
from jax import lax
from jax.experimental import pallas as pl
from jax.experimental.pallas import tpu as pltpu
from jax.sharding import PartitionSpec as P

NY, NX, NZ = 4, 4, 8
SIZE = {"x": NX, "z": NZ, "y": NY}
MESH = pl.DeviceIdType.MESH
HIGHEST = lax.Precision.HIGHEST


PARTS = (("x", "y"), ("y", "x"))
PIECE = 16
BLOCKS = 4
FAR_FIRST = (2, 1, 3)
NEAR_FIRST = (1, 3, 2)
Z_FAR_FIRST = (4, 3, 5, 2, 6, 1, 7)
Z_NEAR_FIRST = Z_FAR_FIRST[::-1]
SCALE = 2.0**17


def dot(a, b, contract, precision=None):
    return lax.dot_general(
        a, b, ((contract[:1], contract[1:]), ((), ())),
        precision=precision, preferred_element_type=jnp.float32,
    )


def encode(value):
    scaled = value * SCALE
    return (scaled * scaled * (scaled * jnp.abs(scaled))).astype(jnp.bfloat16)


def decode(code):
    wide = code.astype(jnp.float32)
    power = jnp.maximum(jnp.abs(wide), 1e-37)
    root = lax.rsqrt(power)
    return wide * root * (lax.rsqrt(power * root) * (1.0 / SCALE))


def exchange_kernel(
    v_hbm, b_hbm, p_hbm, g_ref,
    p_ref, v, v_sib, b, b_sib, early, total, coded, in_far, in_near, in_second, in_z, gathered,
    gram_in, gram_chip, gram_parts, gram_z, gram_row,
    load_sem, sib_send, sib_recv, far_send, far_recv, near_send, near_recv, second_send, second_recv,
    z_send, z_recv, out_z_send, out_z_recv, out_second_send, out_second_recv,
    out_first_send, out_first_recv, fwd_send, fwd_recv, gx_send, gx_recv,
):
    me = lax.axis_index("rows")
    core = me % 2
    mine = {"z": me // 2 % NZ, "x": me // (2 * NZ) % NX, "y": me // (2 * NZ * NX)}

    def device(**moved):
        at = {**mine, "core": core, **moved}
        return (((at["y"] * NX + at["x"]) * NZ + at["z"]) * 2 + at["core"],)

    def along(axis, offset):
        return (mine[axis] + offset + SIZE[axis]) % SIZE[axis]

    sibling = device(core=1 - core)

    def remote(source, target, send, recv, to):
        return pltpu.make_async_remote_copy(
            src_ref=source, dst_ref=target, send_sem=send, recv_sem=recv,
            device_id=to, device_id_type=MESH,
        )

    sends = []

    def start(copy):
        copy.start()
        sends.append(copy)

    half = v_sib.shape[1]
    wide = half // (2 * NX)

    def columns(which_core, group, k):
        return pl.ds(pl.multiple_of(which_core * half + (2 * k + group) * wide, 128), wide)

    apart = (mine["y"] - mine["x"] + 4) % 4
    same, three = 1 - (apart + 3) // 4, apart % 2 * (apart // 2)
    one, two = apart % 2 * (1 - apart // 2), (1 - apart % 2) * (apart // 2)
    offsets = (2, same + 3 * one + three, 3 * same + one + two + 3 * three, 3 * two)
    order = [(group, along("x", offset)) for group in range(2) for offset in offsets]
    loads = []
    for group, k in order:
        loads.append(pltpu.make_async_copy(
            v_hbm.at[:, columns(core, group, k)], v.at[:, columns(core, group, k)], load_sem.at[len(loads)]))
    others = pl.ds(pl.multiple_of((1 - core) * half, 128), half)
    loads.append(pltpu.make_async_copy(v_hbm.at[:, others], v.at[:, others], load_sem.at[len(loads)]))
    load_b = pltpu.make_async_copy(b_hbm, b, load_sem.at[len(loads)])
    load_b.start()
    for load in loads:
        load.start()

    partners = [sibling]
    for dy in range(NY):
        for dx in range(NX):
            if dy or dx:
                partners.append(device(y=along("y", dy), x=along("x", dx)))
    for dz in range(1, NZ):
        partners.append(device(z=along("z", dz)))
    barrier = pltpu.get_barrier_semaphore()
    for partner in partners:
        pl.semaphore_signal(barrier, inc=1, device_id=partner, device_id_type=MESH)
    pl.semaphore_wait(barrier, len(partners))

    copy_b = remote(b_hbm, b_sib, sib_send.at[8], sib_recv.at[8], sibling)
    start(copy_b)
    copies_v = []
    for n, (group, k) in enumerate(order):
        copy = remote(
            v_hbm.at[:, columns(1 - core, group, k)], v_sib.at[:, pl.ds(n * wide, wide)],
            sib_send.at[n], sib_recv.at[n], sibling)
        start(copy)
        copies_v.append(copy)

    load_b.wait()
    b_t = b[...].T
    for n in range(4):
        loads[n].wait()
        early[n] = dot(b_t, v[:, columns(core, *order[n])], (1, 0))
    copy_b.wait_recv()
    b_sib_t = b_sib[...].T

    def far_copy(group, part, way):
        first, _ = PARTS[part]
        return remote(
            coded.at[group, part, along(first, 2), pl.ds(2 * way, 2)], in_far.at[group, part, way],
            far_send.at[group, part, way], far_recv.at[group, part, way],
            device(**{first: along(first, 1 - 2 * way)}))

    def near_copy(group, part, way, relay):
        first, _ = PARTS[part]
        k = along(first, 1 - 2 * way)
        half_of = pl.ds(2 * way if relay else 2 - 2 * way, 2)
        slot = 2 * way + relay
        return remote(
            coded.at[group, part, k, half_of], in_near.at[group, part, way, half_of],
            near_send.at[group, part, slot], near_recv.at[group, part, slot], device(**{first: k}))

    def relay(group):
        for part, (first, _) in enumerate(PARTS):
            for way in range(2):
                far_copy(group, part, way).wait_recv()
                at = (group, part, along(first, 1 - 2 * way), pl.ds(2 * way, 2))
                coded[at] = encode(total[at] + decode(in_far[group, part, way]))
                near_copy(group, part, way, 1).start()

    for n, (group, k) in enumerate(order):
        if group:
            loads[n].wait()
            product = dot(b_t, v[:, columns(core, group, k)], (1, 0))
        else:
            product = early[n]
        copies_v[n].wait_recv()
        product += dot(b_sib_t, v_sib[:, n * wide:(n + 1) * wide], (1, 0))
        for part in range(2):
            for z in range(NZ):
                for o2 in range(4):
                    rank = part * 128 + z % 2 * 64 + o2 * PIECE
                    tile = product[rank:rank + PIECE, z // 2 * 128:(z // 2 + 1) * 128]
                    total[group, part, k, o2, z] = tile
                    coded[group, part, k, o2, z] = encode(tile)
        for part, (first, _) in enumerate(PARTS):
            away = (k - mine[first] + 4) % 4

            @pl.when(away == 2)
            def _():
                for way in range(2):
                    far_copy(group, part, way).start()

            @pl.when(away % 2 == 1)
            def _():
                near_copy(group, part, away // 2, 0).start()
        if n == 5:
            relay(0)
    relay(1)

    def sum_first(group):
        for part, (first, second) in enumerate(PARTS):
            for way in range(2):
                for kind in range(2):
                    near_copy(group, part, way, kind).wait_recv()
            for j2 in FAR_FIRST + (0,):
                o2 = along(second, j2)
                block = total[group, part, mine[first], o2]
                for way in range(2):
                    block += decode(in_near[group, part, way, o2])
                if j2:
                    coded[group, part, mine[first], o2] = encode(block)
                    start(remote(
                        coded.at[group, part, mine[first], o2], in_second.at[group, part, j2 - 1],
                        second_send.at[group, part, j2 - 1], second_recv.at[group, part, j2 - 1],
                        device(**{second: o2})))
                else:
                    total[group, part, mine[first], o2] = block

    def sum_second(group):
        for part, (first, second) in enumerate(PARTS):
            at = (group, part, mine[first], mine[second])
            block = total[at]
            for j2 in FAR_FIRST:
                slot = in_second.at[group, part, j2 - 1]
                remote(
                    slot, slot, second_send.at[group, part, j2 - 1], second_recv.at[group, part, j2 - 1], sibling
                ).wait_recv()
                block += decode(in_second[group, part, j2 - 1])
            total[at] = block
            coded[at] = encode(block)
            for dz in Z_FAR_FIRST:
                z = along("z", dz)
                start(remote(
                    coded.at[at + (z,)], in_z.at[group, part, dz - 1],
                    z_send.at[group, part, dz - 1], z_recv.at[group, part, dz - 1], device(z=z)))

    def spread_z(group):
        for part, (first, second) in enumerate(PARTS):
            piece = total[group, part, mine[first], mine[second], mine["z"]]
            for dz in Z_NEAR_FIRST:
                slot = in_z.at[group, part, dz - 1]
                remote(
                    slot, slot, z_send.at[group, part, dz - 1], z_recv.at[group, part, dz - 1], sibling
                ).wait_recv()
                piece += decode(in_z[group, part, dz - 1])
            here = gathered.at[core, group, part, mine[first], mine[second], mine["z"]]
            here[...] = piece.astype(jnp.bfloat16)
            for dz in Z_FAR_FIRST:
                start(remote(
                    here, here, out_z_send.at[group, part, dz - 1], out_z_recv.at[group, part, dz - 1],
                    device(z=along("z", dz))))

    def spread_second(group):
        for part, (first, second) in enumerate(PARTS):
            for dz in Z_NEAR_FIRST:
                there = gathered.at[core, group, part, mine[first], mine[second], along("z", -dz)]
                remote(
                    there, there, out_z_send.at[group, part, dz - 1], out_z_recv.at[group, part, dz - 1], sibling
                ).wait_recv()
            block = gathered.at[core, group, part, mine[first], mine[second]]
            for j2 in FAR_FIRST:
                start(remote(
                    block, block, out_second_send.at[group, part, j2 - 1],
                    out_second_recv.at[group, part, j2 - 1], device(**{second: along(second, j2)})))

    def forward(group, part, away):
        block = gathered.at[core, group, part, along(PARTS[part][0], -away)]
        start(remote(
            block, block, fwd_send.at[group, part, away], fwd_recv.at[group, part, away], sibling))

    def spread_first(group):
        for part, (first, second) in enumerate(PARTS):
            for j2 in NEAR_FIRST:
                there = gathered.at[core, group, part, mine[first], along(second, -j2)]
                remote(
                    there, there, out_second_send.at[group, part, j2 - 1],
                    out_second_recv.at[group, part, j2 - 1], sibling
                ).wait_recv()
            block = gathered.at[core, group, part, mine[first]]
            for away in FAR_FIRST:
                start(remote(
                    block, block, out_first_send.at[group, part, away - 1],
                    out_first_recv.at[group, part, away - 1], device(**{first: along(first, away)})))
            forward(group, part, 0)

    def add_chunk(which, group, part, away):
        k = along(PARTS[part][0], -away)
        ranks = jnp.concatenate([
            jnp.concatenate([
                gathered[which, group, part, k, :, 2 * n + h].reshape(4 * PIECE, 128) for h in range(2)
            ], axis=0)
            for n in range(BLOCKS)
        ], axis=1)
        term = dot(v[:, columns(which, group, k)], ranks, (1, 1))
        p_ref[:, part * 128:(part + 1) * 128] += term

    def from_chip(group, away):
        for part, (first, second) in enumerate(PARTS):
            if away:
                there = gathered.at[core, group, part, along(first, -away)]
                remote(
                    there, there, out_first_send.at[group, part, away - 1],
                    out_first_recv.at[group, part, away - 1], sibling
                ).wait_recv()
                forward(group, part, away)
        for part in range(2):
            add_chunk(core, group, part, away)

    def from_sibling(group, away):
        for part, (first, second) in enumerate(PARTS):
            there = gathered.at[1 - core, group, part, along(first, -away)]
            remote(
                there, there, fwd_send.at[group, part, away], fwd_recv.at[group, part, away], sibling
            ).wait_recv()
            add_chunk(1 - core, group, part, away)

    sum_first(0)
    sum_second(0)
    sum_first(1)
    spread_z(0)
    sum_second(1)
    spread_second(0)
    spread_z(1)
    spread_first(0)
    p_ref[...] = jnp.zeros_like(p_ref)
    loads[8].wait()
    from_chip(0, 0)
    spread_second(1)
    from_sibling(0, 0)
    from_chip(0, 2)
    spread_first(1)
    from_chip(0, 1)
    from_sibling(0, 2)
    from_chip(0, 3)
    from_chip(1, 0)
    from_sibling(0, 1)
    from_sibling(0, 3)
    from_sibling(1, 0)
    from_chip(1, 2)
    from_chip(1, 1)
    from_sibling(1, 2)
    from_chip(1, 3)
    from_sibling(1, 1)
    from_sibling(1, 3)

    projected = p_ref[...]
    store = pltpu.make_async_copy(p_ref, p_hbm, load_sem.at[10])
    store.start()
    gram_in[0] = dot(projected, projected, (0, 0), HIGHEST)

    copy = remote(gram_in.at[0], gram_in.at[1], gx_send.at[0], gx_recv.at[0], sibling)
    start(copy)
    copy.wait_recv()
    gram_chip[...] = (gram_in[0] + gram_in[1]).reshape(NY, NX, 16, 256)

    plane = [(dy, dx) for dy in (2, 1, 3, 0) for dx in (2, 1, 3, 0) if dy or dx]
    scatter = []
    for n, (dy, dx) in enumerate(plane):
        y, x = along("y", dy), along("x", dx)
        copy = remote(
            gram_chip.at[y, x], gram_parts.at[n], gx_send.at[1 + n], gx_recv.at[1 + n], device(y=y, x=x))
        start(copy)
        scatter.append(copy)
    row = gram_chip[mine["y"], mine["x"]]
    for n, copy in reversed(list(enumerate(scatter))):
        copy.wait_recv()
        row += gram_parts[n]
    gram_z[mine["z"]] = row
    for dz in Z_FAR_FIRST:
        slot = 16 + dz
        here = gram_z.at[mine["z"]]
        start(remote(here, here, gx_send.at[slot], gx_recv.at[slot], device(z=along("z", dz))))
    for dz in Z_NEAR_FIRST:
        slot = 16 + dz
        there = gram_z.at[along("z", -dz)]
        remote(there, there, gx_send.at[slot], gx_recv.at[slot], sibling).wait_recv()
    row = gram_z[0]
    for n in range(1, NZ):
        row += gram_z[n]
    gram_row[mine["y"], mine["x"]] = row
    for n, (dy, dx) in enumerate(plane):
        slot = 24 + n
        here = gram_row.at[mine["y"], mine["x"]]
        start(remote(
            here, here, gx_send.at[slot], gx_recv.at[slot], device(y=along("y", dy), x=along("x", dx))))
    for n, (dy, dx) in enumerate(plane):
        slot = 24 + n
        there = gram_row.at[along("y", -dy), along("x", -dx)]
        remote(there, there, gx_send.at[slot], gx_recv.at[slot], sibling).wait_recv()
    g_ref[...] = gram_row[...].reshape(256, 256)
    store.wait()
    for group in range(2):
        for part in range(2):
            for way in range(2):
                far_copy(group, part, way).wait_send()
                for kind in range(2):
                    near_copy(group, part, way, kind).wait_send()
    for copy in sends:
        copy.wait_send()


def exchange(velocity, basis_in):
    rows, snaps = velocity.shape
    rank = basis_in.shape[1]
    f32, bf16 = jnp.float32, jnp.bfloat16

    def pair(*shape):
        return [pltpu.SemaphoreType.DMA(shape)] * 2

    return pl.pallas_call(
        exchange_kernel,
        out_shape=(
            jax.ShapeDtypeStruct((rows, rank), f32),
            jax.ShapeDtypeStruct((rank, rank), f32),
        ),
        in_specs=[pl.BlockSpec(memory_space=pltpu.HBM)] * 2,
        out_specs=[pl.BlockSpec(memory_space=pl.ANY), pl.BlockSpec(memory_space=pltpu.VMEM)],
        scratch_shapes=[
            pltpu.VMEM((rows, rank), f32),
            pltpu.VMEM((rows, snaps), bf16),
            pltpu.VMEM((rows, snaps // 2), bf16),
            pltpu.VMEM((rows, rank), bf16),
            pltpu.VMEM((rows, rank), bf16),
            pltpu.VMEM((4, rank, snaps // 16), f32),
            pltpu.VMEM((2, 2, 4, 4, NZ, PIECE, 128), f32),
            pltpu.VMEM((2, 2, 4, 4, NZ, PIECE, 128), bf16),
            pltpu.VMEM((2, 2, 2, 2, NZ, PIECE, 128), bf16),
            pltpu.VMEM((2, 2, 2, 4, NZ, PIECE, 128), bf16),
            pltpu.VMEM((2, 2, 3, NZ, PIECE, 128), bf16),
            pltpu.VMEM((2, 2, NZ - 1, PIECE, 128), bf16),
            pltpu.VMEM((2, 2, 2, 4, 4, NZ, PIECE, 128), bf16),
            pltpu.VMEM((2, rank, rank), f32),
            pltpu.VMEM((NY, NX, 16, rank), f32),
            pltpu.VMEM((NY * NX - 1, 16, rank), f32),
            pltpu.VMEM((NZ, 16, rank), f32),
            pltpu.VMEM((NY, NX, 16, rank), f32),
            pltpu.SemaphoreType.DMA((11,)),
            *pair(9),
            *pair(2, 2, 2),
            *pair(2, 2, 4),
            *pair(2, 2, 3),
            *pair(2, 2, NZ - 1),
            *pair(2, 2, NZ - 1),
            *pair(2, 2, 3),
            *pair(2, 2, 3),
            *pair(2, 2, 4),
            *pair(39),
        ],
        compiler_params=pltpu.CompilerParams(
            collective_id=0, has_side_effects=True, vmem_limit_bytes=107 * 2**19
        ),
        cost_estimate=pl.CostEstimate(
            flops=4 * rows * snaps * rank, bytes_accessed=2 * rows * snaps, transcendentals=0
        ),
    )(velocity, basis_in)


def split_dot(a, b):
    a_high, b_high = a.astype(jnp.bfloat16), b.astype(jnp.bfloat16)
    a_low = (a - a_high.astype(jnp.float32)).astype(jnp.bfloat16)
    b_low = (b - b_high.astype(jnp.float32)).astype(jnp.bfloat16)
    return dot(a_high, b_high, (1, 0)) + (dot(a_high, b_low, (1, 0)) + dot(a_low, b_high, (1, 0)))


def factor_kernel(scale, p_hbm, g_ref, out_hbm, r_hbm, p_ref, out, r_ref, moved, state, sem):
    load = pltpu.make_async_copy(p_hbm, p_ref, sem.at[5])
    load.start()
    size = g_ref.shape[0]
    bf16 = jnp.bfloat16
    row = lax.broadcasted_iota(jnp.int32, (size, size), 0)
    col = lax.broadcasted_iota(jnp.int32, (size, size), 1)
    eye = (row == col).astype(jnp.float32)
    weight = jnp.where(row < col, 1.0, 0.5 * eye)
    gram = g_ref[...]
    diagonal = gram * eye
    unit_row = lax.rsqrt(jnp.sum(diagonal, axis=0, keepdims=True))
    unit_col = lax.rsqrt(jnp.sum(diagonal, axis=1, keepdims=True))
    scaled = gram * unit_row * unit_col
    excess = scaled - eye

    def refine(u):
        small = u.astype(bf16)
        return u - weight * dot(small, small, (0, 0))

    def advance(d, u, exact):
        x = refine(u) if exact else u
        small = x.astype(bf16)
        y = x - dot(small, small, (1, 0))
        if exact:
            return d - y - dot(d, y, (1, 0), HIGHEST)
        return d - y - dot(d.astype(bf16), y.astype(bf16), (1, 0))

    def rest(d, exact):
        if exact:
            once = excess + dot(excess, d, (1, 0), HIGHEST)
            return weight * (once + dot(d, d + once, (0, 0), HIGHEST)) + d
        near = d.astype(bf16)
        once = excess + dot(excess.astype(bf16), near, (1, 0))
        return weight * (once + dot(near, (d + once).astype(bf16), (0, 0))) + d

    x = refine(weight * excess)
    small = x.astype(bf16)
    square = dot(small, small, (1, 0))
    d = square - x - dot(square.astype(bf16), small, (1, 0))
    d = advance(d, rest(d, False), False)
    u = rest(d, True)
    moved[...] = d
    state[...] = u

    def go_on(carry):
        count, norm = carry
        return (norm > 2e-5) & (norm < 1e4) & (count < 12)

    def step(carry):
        count, _ = carry
        d = advance(moved[...], state[...], True)
        u = rest(d, True)
        moved[...] = d
        state[...] = u
        return count + 1, jnp.sum(u * u)

    _, norm = lax.while_loop(go_on, step, (0, jnp.sum(u * u)))
    converged = norm <= 2e-5

    @pl.when(converged)
    def _():
        moved[...] = advance(moved[...], state[...], True)

    @pl.when(jnp.logical_not(converged))
    def _():
        state[...] = scaled
        r_ref[...] = jnp.zeros_like(r_ref)
        lane = lax.broadcasted_iota(jnp.int32, (1, size), 1)

        def eliminate(j, _):
            pivot_row = jnp.where(lane >= j, state[pl.ds(j, 1), :], 0.0)
            pivot = jnp.sum(jnp.where(lane == j, pivot_row, 0.0), axis=1, keepdims=True)
            pivot_row = pivot_row / jnp.sqrt(pivot)
            r_ref[pl.ds(j, 1), :] = pivot_row
            pivot_col = jnp.sum(jnp.broadcast_to(pivot_row, (size, size)) * eye, axis=1, keepdims=True)
            state[...] = state[...] - pivot_col * pivot_row
            return 0

        lax.fori_loop(0, size, eliminate, 0)
        moved[...] = jnp.zeros_like(moved)

        def substitute(n, _):
            j = size - 1 - n
            line = r_ref[pl.ds(j, 1), :]
            pivot = jnp.sum(jnp.where(lane == j, line, 0.0), axis=1, keepdims=True)
            beyond = jnp.where(lane > j, line, 0.0)
            unit = jnp.where(lane == j, 1.0, 0.0)
            moved[pl.ds(j, 1), :] = (unit - dot(beyond, moved[...], (1, 0), HIGHEST)) / pivot
            return 0

        lax.fori_loop(0, size, substitute, 0)
        moved[...] = moved[...] - eye

    d = moved[...]
    load.wait()
    copies = []
    rows = p_ref.shape[0] // 4
    for n in range(4):
        block = pl.ds(n * rows, rows)
        p = p_ref[block, :] * (unit_row * scale)
        out[block, :] = p + split_dot(p, d)
        copy = pltpu.make_async_copy(out.at[block, :], out_hbm.at[block, :], sem.at[n])
        copy.start()
        copies.append(copy)
    triangle = jnp.where(row <= col, scaled + dot(d, scaled, (0, 0), HIGHEST), 0.0)
    r_ref[...] = triangle / (unit_row * scale)
    copy = pltpu.make_async_copy(r_ref, r_hbm, sem.at[4])
    copy.start()
    copies.append(copy)
    for copy in copies:
        copy.wait()


def factor(projected, gram, scale):
    rank = gram.shape[0]
    return pl.pallas_call(
        functools.partial(factor_kernel, scale),
        out_shape=(
            jax.ShapeDtypeStruct(projected.shape, jnp.float32),
            jax.ShapeDtypeStruct((rank, rank), jnp.float32),
        ),
        in_specs=[pl.BlockSpec(memory_space=pl.ANY), pl.BlockSpec(memory_space=pltpu.VMEM)],
        out_specs=[pl.BlockSpec(memory_space=pl.ANY)] * 2,
        scratch_shapes=[
            *[pltpu.VMEM(projected.shape, jnp.float32)] * 2,
            *[pltpu.VMEM((rank, rank), jnp.float32)] * 3,
            pltpu.SemaphoreType.DMA((6,)),
        ],
        compiler_params=pltpu.CompilerParams(vmem_limit_bytes=107 * 2**19),
    )(projected, gram)


def local(velocity, basis_in):
    projected, gram = exchange(velocity, basis_in)
    scale = float(lax.axis_size("rows") * velocity.shape[0]) ** 0.5
    return factor(projected, gram, scale)


def solution(mesh):
    in_specs = (P("rows", None), P("rows", None))
    out_specs = (P("rows", None), P())
    return jax.shard_map(local, mesh=mesh, in_specs=in_specs, out_specs=out_specs, check_vma=False)
```

```python
import functools

import jax
import jax.numpy as jnp
from jax import lax
from jax.experimental import pallas as pl
from jax.experimental.pallas import tpu as pltpu
from jax.sharding import PartitionSpec as P

NY, NX, NZ = 4, 4, 8
SIZE = {"x": NX, "z": NZ, "y": NY}
MESH = pl.DeviceIdType.MESH
HIGHEST = lax.Precision.HIGHEST


PARTS = (("x", "y"), ("y", "x"))
PIECE = 16
BLOCKS = 4
FAR_FIRST = (2, 1, 3)
NEAR_FIRST = (1, 3, 2)
Z_FAR_FIRST = (4, 3, 5, 2, 6, 1, 7)
Z_NEAR_FIRST = Z_FAR_FIRST[::-1]
SCALE = 2.0**17


def dot(a, b, contract, precision=None):
    return lax.dot_general(
        a, b, ((contract[:1], contract[1:]), ((), ())),
        precision=precision, preferred_element_type=jnp.float32,
    )


def encode(value):
    scaled = value * SCALE
    return (scaled * scaled * (scaled * jnp.abs(scaled))).astype(jnp.bfloat16)


def decode(code):
    wide = code.astype(jnp.float32)
    power = jnp.maximum(jnp.abs(wide), 1e-37)
    root = lax.rsqrt(power)
    return wide * root * (lax.rsqrt(power * root) * (1.0 / SCALE))


def exchange_kernel(
    v_hbm, b_hbm, p_hbm, g_ref,
    p_ref, v, v_sib, b, b_sib, early, total, coded, in_far, in_near, in_second, in_z, gathered,
    gram_in, gram_chip, gram_parts, gram_z, gram_row,
    load_sem, sib_send, sib_recv, far_send, far_recv, near_send, near_recv, second_send, second_recv,
    z_send, z_recv, out_z_send, out_z_recv, out_second_send, out_second_recv,
    out_first_send, out_first_recv, fwd_send, fwd_recv, gx_send, gx_recv,
):
    me = lax.axis_index("rows")
    core = me % 2
    mine = {"z": me // 2 % NZ, "x": me // (2 * NZ) % NX, "y": me // (2 * NZ * NX)}

    def device(**moved):
        at = {**mine, "core": core, **moved}
        return (((at["y"] * NX + at["x"]) * NZ + at["z"]) * 2 + at["core"],)

    def along(axis, offset):
        return (mine[axis] + offset + SIZE[axis]) % SIZE[axis]

    sibling = device(core=1 - core)

    def remote(source, target, send, recv, to):
        return pltpu.make_async_remote_copy(
            src_ref=source, dst_ref=target, send_sem=send, recv_sem=recv,
            device_id=to, device_id_type=MESH,
        )

    sends = []

    def start(copy):
        copy.start()
        sends.append(copy)

    def settle():
        for copy in sends:
            copy.wait_send()
        sends.clear()

    half = v_sib.shape[1]
    wide = half // (2 * NX)

    def columns(which_core, group, k):
        return pl.ds(pl.multiple_of(which_core * half + (2 * k + group) * wide, 128), wide)

    apart = (mine["y"] - mine["x"] + 4) % 4
    same, three = 1 - (apart + 3) // 4, apart % 2 * (apart // 2)
    one, two = apart % 2 * (1 - apart // 2), (1 - apart % 2) * (apart // 2)
    offsets = (2, same + 3 * one + three, 3 * same + one + two + 3 * three, 3 * two)
    order = [(group, along("x", offset)) for group in range(2) for offset in offsets]
    loads = []
    for group, k in order:
        loads.append(pltpu.make_async_copy(
            v_hbm.at[:, columns(core, group, k)], v.at[:, columns(core, group, k)], load_sem.at[len(loads)]))
    others = pl.ds(pl.multiple_of((1 - core) * half, 128), half)
    loads.append(pltpu.make_async_copy(v_hbm.at[:, others], v.at[:, others], load_sem.at[len(loads)]))
    load_b = pltpu.make_async_copy(b_hbm, b, load_sem.at[len(loads)])
    load_b.start()
    for load in loads:
        load.start()

    partners = [sibling]
    for dy in range(NY):
        for dx in range(NX):
            if dy or dx:
                partners.append(device(y=along("y", dy), x=along("x", dx)))
    for dz in range(1, NZ):
        partners.append(device(z=along("z", dz)))
    barrier = pltpu.get_barrier_semaphore()
    for partner in partners:
        pl.semaphore_signal(barrier, inc=1, device_id=partner, device_id_type=MESH)
    pl.semaphore_wait(barrier, len(partners))

    copy_b = remote(b_hbm, b_sib, sib_send.at[8], sib_recv.at[8], sibling)
    start(copy_b)
    copies_v = []
    for n, (group, k) in enumerate(order):
        copy = remote(
            v_hbm.at[:, columns(1 - core, group, k)], v_sib.at[:, pl.ds(n * wide, wide)],
            sib_send.at[n], sib_recv.at[n], sibling)
        start(copy)
        copies_v.append(copy)

    load_b.wait()
    b_t = b[...].T
    for n in range(4):
        loads[n].wait()
        early[n] = dot(b_t, v[:, columns(core, *order[n])], (1, 0))
    copy_b.wait_recv()
    b_sib_t = b_sib[...].T

    def far_copy(group, part, way):
        first, _ = PARTS[part]
        return remote(
            coded.at[group, part, along(first, 2), pl.ds(2 * way, 2)], in_far.at[group, part, way],
            far_send.at[group, part, way], far_recv.at[group, part, way],
            device(**{first: along(first, 1 - 2 * way)}))

    def near_copy(group, part, way, relay):
        first, _ = PARTS[part]
        k = along(first, 1 - 2 * way)
        half_of = pl.ds(2 * way if relay else 2 - 2 * way, 2)
        slot = 2 * way + relay
        return remote(
            coded.at[group, part, k, half_of], in_near.at[group, part, way, half_of],
            near_send.at[group, part, slot], near_recv.at[group, part, slot], device(**{first: k}))

    def relay(group):
        for part, (first, _) in enumerate(PARTS):
            for way in range(2):
                far_copy(group, part, way).wait_recv()
                at = (group, part, along(first, 1 - 2 * way), pl.ds(2 * way, 2))
                coded[at] = encode(total[at] + decode(in_far[group, part, way]))
                near_copy(group, part, way, 1).start()

    for n, (group, k) in enumerate(order):
        if group:
            loads[n].wait()
            product = dot(b_t, v[:, columns(core, group, k)], (1, 0))
        else:
            product = early[n]
        copies_v[n].wait_recv()
        product += dot(b_sib_t, v_sib[:, n * wide:(n + 1) * wide], (1, 0))
        for part in range(2):
            for z in range(NZ):
                for o2 in range(4):
                    rank = part * 128 + z % 2 * 64 + o2 * PIECE
                    tile = product[rank:rank + PIECE, z // 2 * 128:(z // 2 + 1) * 128]
                    total[group, part, k, o2, z] = tile
                    coded[group, part, k, o2, z] = encode(tile)
        for part, (first, _) in enumerate(PARTS):
            away = (k - mine[first] + 4) % 4

            @pl.when(away == 2)
            def _():
                for way in range(2):
                    far_copy(group, part, way).start()

            @pl.when(away % 2 == 1)
            def _():
                near_copy(group, part, away // 2, 0).start()
        if n == 5:
            relay(0)
    relay(1)

    def sum_first(group):
        for part, (first, second) in enumerate(PARTS):
            for way in range(2):
                for kind in range(2):
                    near_copy(group, part, way, kind).wait_recv()
            for j2 in FAR_FIRST + (0,):
                o2 = along(second, j2)
                block = total[group, part, mine[first], o2]
                for way in range(2):
                    block += decode(in_near[group, part, way, o2])
                if j2:
                    coded[group, part, mine[first], o2] = encode(block)
                    start(remote(
                        coded.at[group, part, mine[first], o2], in_second.at[group, part, j2 - 1],
                        second_send.at[group, part, j2 - 1], second_recv.at[group, part, j2 - 1],
                        device(**{second: o2})))
                else:
                    total[group, part, mine[first], o2] = block

    def sum_second(group):
        for part, (first, second) in enumerate(PARTS):
            at = (group, part, mine[first], mine[second])
            block = total[at]
            for j2 in FAR_FIRST:
                slot = in_second.at[group, part, j2 - 1]
                remote(
                    slot, slot, second_send.at[group, part, j2 - 1], second_recv.at[group, part, j2 - 1], sibling
                ).wait_recv()
                block += decode(in_second[group, part, j2 - 1])
            total[at] = block
            coded[at] = encode(block)
            for dz in Z_FAR_FIRST:
                z = along("z", dz)
                start(remote(
                    coded.at[at + (z,)], in_z.at[group, part, dz - 1],
                    z_send.at[group, part, dz - 1], z_recv.at[group, part, dz - 1], device(z=z)))

    def spread_z(group):
        for part, (first, second) in enumerate(PARTS):
            piece = total[group, part, mine[first], mine[second], mine["z"]]
            for dz in Z_NEAR_FIRST:
                slot = in_z.at[group, part, dz - 1]
                remote(
                    slot, slot, z_send.at[group, part, dz - 1], z_recv.at[group, part, dz - 1], sibling
                ).wait_recv()
                piece += decode(in_z[group, part, dz - 1])
            here = gathered.at[core, group, part, mine[first], mine[second], mine["z"]]
            here[...] = piece.astype(jnp.bfloat16)
            for dz in Z_FAR_FIRST:
                start(remote(
                    here, here, out_z_send.at[group, part, dz - 1], out_z_recv.at[group, part, dz - 1],
                    device(z=along("z", dz))))

    def spread_second(group):
        for part, (first, second) in enumerate(PARTS):
            for dz in Z_NEAR_FIRST:
                there = gathered.at[core, group, part, mine[first], mine[second], along("z", -dz)]
                remote(
                    there, there, out_z_send.at[group, part, dz - 1], out_z_recv.at[group, part, dz - 1], sibling
                ).wait_recv()
            block = gathered.at[core, group, part, mine[first], mine[second]]
            for j2 in FAR_FIRST:
                start(remote(
                    block, block, out_second_send.at[group, part, j2 - 1],
                    out_second_recv.at[group, part, j2 - 1], device(**{second: along(second, j2)})))

    def forward(group, part, away):
        block = gathered.at[core, group, part, along(PARTS[part][0], -away)]
        start(remote(
            block, block, fwd_send.at[group, part, away], fwd_recv.at[group, part, away], sibling))

    def spread_first(group):
        for part, (first, second) in enumerate(PARTS):
            for j2 in NEAR_FIRST:
                there = gathered.at[core, group, part, mine[first], along(second, -j2)]
                remote(
                    there, there, out_second_send.at[group, part, j2 - 1],
                    out_second_recv.at[group, part, j2 - 1], sibling
                ).wait_recv()
            block = gathered.at[core, group, part, mine[first]]
            for away in FAR_FIRST:
                start(remote(
                    block, block, out_first_send.at[group, part, away - 1],
                    out_first_recv.at[group, part, away - 1], device(**{first: along(first, away)})))
            forward(group, part, 0)

    def add_chunk(which, group, part, away):
        k = along(PARTS[part][0], -away)
        ranks = jnp.concatenate([
            jnp.concatenate([
                gathered[which, group, part, k, :, 2 * n + h].reshape(4 * PIECE, 128) for h in range(2)
            ], axis=0)
            for n in range(BLOCKS)
        ], axis=1)
        term = dot(v[:, columns(which, group, k)], ranks, (1, 1))
        p_ref[:, part * 128:(part + 1) * 128] += term

    def from_chip(group, away):
        for part, (first, second) in enumerate(PARTS):
            if away:
                there = gathered.at[core, group, part, along(first, -away)]
                remote(
                    there, there, out_first_send.at[group, part, away - 1],
                    out_first_recv.at[group, part, away - 1], sibling
                ).wait_recv()
                forward(group, part, away)
        for part in range(2):
            add_chunk(core, group, part, away)

    def from_sibling(group, away):
        for part, (first, second) in enumerate(PARTS):
            there = gathered.at[1 - core, group, part, along(first, -away)]
            remote(
                there, there, fwd_send.at[group, part, away], fwd_recv.at[group, part, away], sibling
            ).wait_recv()
            add_chunk(1 - core, group, part, away)

    sum_first(0)
    sum_second(0)
    sum_first(1)
    spread_z(0)
    sum_second(1)
    spread_second(0)
    spread_z(1)
    spread_first(0)
    p_ref[...] = jnp.zeros_like(p_ref)
    loads[8].wait()
    from_chip(0, 0)
    spread_second(1)
    from_sibling(0, 0)
    from_chip(0, 2)
    spread_first(1)
    from_chip(0, 1)
    from_sibling(0, 2)
    from_chip(0, 3)
    from_chip(1, 0)
    from_sibling(0, 1)
    from_sibling(0, 3)
    from_sibling(1, 0)
    from_chip(1, 2)
    from_chip(1, 1)
    from_sibling(1, 2)
    from_chip(1, 3)
    from_sibling(1, 1)
    from_sibling(1, 3)

    projected = p_ref[...]
    store = pltpu.make_async_copy(p_ref, p_hbm, load_sem.at[10])
    store.start()
    gram_in[0] = dot(projected, projected, (0, 0), HIGHEST)

    copy = remote(gram_in.at[0], gram_in.at[1], gx_send.at[0], gx_recv.at[0], sibling)
    start(copy)
    copy.wait_recv()
    gram_chip[...] = (gram_in[0] + gram_in[1]).reshape(NY, NX, 16, 256)

    plane = [(dy, dx) for dy in (2, 1, 3, 0) for dx in (2, 1, 3, 0) if dy or dx]
    scatter = []
    for n, (dy, dx) in enumerate(plane):
        y, x = along("y", dy), along("x", dx)
        copy = remote(
            gram_chip.at[y, x], gram_parts.at[n], gx_send.at[1 + n], gx_recv.at[1 + n], device(y=y, x=x))
        copy.start()
        scatter.append(copy)

    for group in range(2):
        for part in range(2):
            for way in range(2):
                far_copy(group, part, way).wait_send()
                for kind in range(2):
                    near_copy(group, part, way, kind).wait_send()
    settle()
    store.wait()
    row = gram_chip[mine["y"], mine["x"]]
    for n, copy in reversed(list(enumerate(scatter))):
        copy.wait_recv()
        row += gram_parts[n]
    gram_z[mine["z"]] = row
    for dz in Z_FAR_FIRST:
        slot = 16 + dz
        here = gram_z.at[mine["z"]]
        start(remote(here, here, gx_send.at[slot], gx_recv.at[slot], device(z=along("z", dz))))
    for copy in scatter:
        copy.wait_send()
    for dz in Z_NEAR_FIRST:
        slot = 16 + dz
        there = gram_z.at[along("z", -dz)]
        remote(there, there, gx_send.at[slot], gx_recv.at[slot], sibling).wait_recv()
    settle()
    row = gram_z[0]
    for n in range(1, NZ):
        row += gram_z[n]
    gram_row[mine["y"], mine["x"]] = row
    for n, (dy, dx) in enumerate(plane):
        slot = 24 + n
        here = gram_row.at[mine["y"], mine["x"]]
        start(remote(
            here, here, gx_send.at[slot], gx_recv.at[slot], device(y=along("y", dy), x=along("x", dx))))
    for n, (dy, dx) in enumerate(plane):
        slot = 24 + n
        there = gram_row.at[along("y", -dy), along("x", -dx)]
        remote(there, there, gx_send.at[slot], gx_recv.at[slot], sibling).wait_recv()
    g_ref[...] = gram_row[...].reshape(256, 256)
    settle()


def exchange(velocity, basis_in):
    rows, snaps = velocity.shape
    rank = basis_in.shape[1]
    f32, bf16 = jnp.float32, jnp.bfloat16

    def pair(*shape):
        return [pltpu.SemaphoreType.DMA(shape)] * 2

    return pl.pallas_call(
        exchange_kernel,
        out_shape=(
            jax.ShapeDtypeStruct((rows, rank), f32),
            jax.ShapeDtypeStruct((rank, rank), f32),
        ),
        in_specs=[pl.BlockSpec(memory_space=pltpu.HBM)] * 2,
        out_specs=[pl.BlockSpec(memory_space=pl.ANY), pl.BlockSpec(memory_space=pltpu.VMEM)],
        scratch_shapes=[
            pltpu.VMEM((rows, rank), f32),
            pltpu.VMEM((rows, snaps), bf16),
            pltpu.VMEM((rows, snaps // 2), bf16),
            pltpu.VMEM((rows, rank), bf16),
            pltpu.VMEM((rows, rank), bf16),
            pltpu.VMEM((4, rank, snaps // 16), f32),
            pltpu.VMEM((2, 2, 4, 4, NZ, PIECE, 128), f32),
            pltpu.VMEM((2, 2, 4, 4, NZ, PIECE, 128), bf16),
            pltpu.VMEM((2, 2, 2, 2, NZ, PIECE, 128), bf16),
            pltpu.VMEM((2, 2, 2, 4, NZ, PIECE, 128), bf16),
            pltpu.VMEM((2, 2, 3, NZ, PIECE, 128), bf16),
            pltpu.VMEM((2, 2, NZ - 1, PIECE, 128), bf16),
            pltpu.VMEM((2, 2, 2, 4, 4, NZ, PIECE, 128), bf16),
            pltpu.VMEM((2, rank, rank), f32),
            pltpu.VMEM((NY, NX, 16, rank), f32),
            pltpu.VMEM((NY * NX - 1, 16, rank), f32),
            pltpu.VMEM((NZ, 16, rank), f32),
            pltpu.VMEM((NY, NX, 16, rank), f32),
            pltpu.SemaphoreType.DMA((11,)),
            *pair(9),
            *pair(2, 2, 2),
            *pair(2, 2, 4),
            *pair(2, 2, 3),
            *pair(2, 2, NZ - 1),
            *pair(2, 2, NZ - 1),
            *pair(2, 2, 3),
            *pair(2, 2, 3),
            *pair(2, 2, 4),
            *pair(39),
        ],
        compiler_params=pltpu.CompilerParams(
            collective_id=0, has_side_effects=True, vmem_limit_bytes=107 * 2**19
        ),
        cost_estimate=pl.CostEstimate(
            flops=4 * rows * snaps * rank, bytes_accessed=2 * rows * snaps, transcendentals=0
        ),
    )(velocity, basis_in)


def split_dot(a, b):
    a_high, b_high = a.astype(jnp.bfloat16), b.astype(jnp.bfloat16)
    a_low = (a - a_high.astype(jnp.float32)).astype(jnp.bfloat16)
    b_low = (b - b_high.astype(jnp.float32)).astype(jnp.bfloat16)
    return dot(a_high, b_high, (1, 0)) + (dot(a_high, b_low, (1, 0)) + dot(a_low, b_high, (1, 0)))


def factor_kernel(scale, p_hbm, g_ref, out_hbm, r_hbm, p_ref, out, r_ref, moved, state, sem):
    load = pltpu.make_async_copy(p_hbm, p_ref, sem.at[5])
    load.start()
    size = g_ref.shape[0]
    bf16 = jnp.bfloat16
    row = lax.broadcasted_iota(jnp.int32, (size, size), 0)
    col = lax.broadcasted_iota(jnp.int32, (size, size), 1)
    eye = (row == col).astype(jnp.float32)
    weight = jnp.where(row < col, 1.0, 0.5 * eye)
    gram = g_ref[...]
    diagonal = gram * eye
    unit_row = lax.rsqrt(jnp.sum(diagonal, axis=0, keepdims=True))
    unit_col = lax.rsqrt(jnp.sum(diagonal, axis=1, keepdims=True))
    scaled = gram * unit_row * unit_col
    excess = scaled - eye

    def refine(u):
        small = u.astype(bf16)
        return u - weight * dot(small, small, (0, 0))

    def advance(d, u, exact):
        x = refine(u) if exact else u
        small = x.astype(bf16)
        y = x - dot(small, small, (1, 0))
        if exact:
            return d - y - dot(d, y, (1, 0), HIGHEST)
        return d - y - dot(d.astype(bf16), y.astype(bf16), (1, 0))

    def rest(d, exact):
        if exact:
            once = excess + dot(excess, d, (1, 0), HIGHEST)
            return weight * (once + dot(d, d + once, (0, 0), HIGHEST)) + d
        near = d.astype(bf16)
        once = excess + dot(excess.astype(bf16), near, (1, 0))
        return weight * (once + dot(near, (d + once).astype(bf16), (0, 0))) + d

    x = refine(weight * excess)
    small = x.astype(bf16)
    square = dot(small, small, (1, 0))
    d = square - x - dot(square.astype(bf16), small, (1, 0))
    d = advance(d, rest(d, False), False)
    u = rest(d, True)
    moved[...] = d
    state[...] = u

    def go_on(carry):
        count, norm = carry
        return (norm > 2e-5) & (norm < 1e4) & (count < 12)

    def step(carry):
        count, _ = carry
        d = advance(moved[...], state[...], True)
        u = rest(d, True)
        moved[...] = d
        state[...] = u
        return count + 1, jnp.sum(u * u)

    _, norm = lax.while_loop(go_on, step, (0, jnp.sum(u * u)))
    converged = norm <= 2e-5

    @pl.when(converged)
    def _():
        moved[...] = advance(moved[...], state[...], True)

    @pl.when(jnp.logical_not(converged))
    def _():
        state[...] = scaled
        r_ref[...] = jnp.zeros_like(r_ref)
        lane = lax.broadcasted_iota(jnp.int32, (1, size), 1)

        def eliminate(j, _):
            pivot_row = jnp.where(lane >= j, state[pl.ds(j, 1), :], 0.0)
            pivot = jnp.sum(jnp.where(lane == j, pivot_row, 0.0), axis=1, keepdims=True)
            pivot_row = pivot_row / jnp.sqrt(pivot)
            r_ref[pl.ds(j, 1), :] = pivot_row
            pivot_col = jnp.sum(jnp.broadcast_to(pivot_row, (size, size)) * eye, axis=1, keepdims=True)
            state[...] = state[...] - pivot_col * pivot_row
            return 0

        lax.fori_loop(0, size, eliminate, 0)
        moved[...] = jnp.zeros_like(moved)

        def substitute(n, _):
            j = size - 1 - n
            line = r_ref[pl.ds(j, 1), :]
            pivot = jnp.sum(jnp.where(lane == j, line, 0.0), axis=1, keepdims=True)
            beyond = jnp.where(lane > j, line, 0.0)
            unit = jnp.where(lane == j, 1.0, 0.0)
            moved[pl.ds(j, 1), :] = (unit - dot(beyond, moved[...], (1, 0), HIGHEST)) / pivot
            return 0

        lax.fori_loop(0, size, substitute, 0)
        moved[...] = moved[...] - eye

    d = moved[...]
    load.wait()
    copies = []
    rows = p_ref.shape[0] // 4
    for n in range(4):
        block = pl.ds(n * rows, rows)
        p = p_ref[block, :] * (unit_row * scale)
        out[block, :] = p + split_dot(p, d)
        copy = pltpu.make_async_copy(out.at[block, :], out_hbm.at[block, :], sem.at[n])
        copy.start()
        copies.append(copy)
    triangle = jnp.where(row <= col, scaled + dot(d, scaled, (0, 0), HIGHEST), 0.0)
    r_ref[...] = triangle / (unit_row * scale)
    copy = pltpu.make_async_copy(r_ref, r_hbm, sem.at[4])
    copy.start()
    copies.append(copy)
    for copy in copies:
        copy.wait()


def factor(projected, gram, scale):
    rank = gram.shape[0]
    return pl.pallas_call(
        functools.partial(factor_kernel, scale),
        out_shape=(
            jax.ShapeDtypeStruct(projected.shape, jnp.float32),
            jax.ShapeDtypeStruct((rank, rank), jnp.float32),
        ),
        in_specs=[pl.BlockSpec(memory_space=pl.ANY), pl.BlockSpec(memory_space=pltpu.VMEM)],
        out_specs=[pl.BlockSpec(memory_space=pl.ANY)] * 2,
        scratch_shapes=[
            *[pltpu.VMEM(projected.shape, jnp.float32)] * 2,
            *[pltpu.VMEM((rank, rank), jnp.float32)] * 3,
            pltpu.SemaphoreType.DMA((6,)),
        ],
        compiler_params=pltpu.CompilerParams(vmem_limit_bytes=107 * 2**19),
    )(projected, gram)


def local(velocity, basis_in):
    projected, gram = exchange(velocity, basis_in)
    scale = float(lax.axis_size("rows") * velocity.shape[0]) ** 0.5
    return factor(projected, gram, scale)


def solution(mesh):
    in_specs = (P("rows", None), P("rows", None))
    out_specs = (P("rows", None), P())
    return jax.shard_map(local, mesh=mesh, in_specs=in_specs, out_specs=out_specs, check_vma=False)
```
